256 devices in a mesh: ctx: 32 (over z, x), head: 8 (over y, core).
Axes of the slice: x: 4, y: 4, z: 8, core: 2. Of those that a mesh axis runs over, the one named last changes fastest.
Arguments:
- self_queries: bfloat16 [4096, 8192], P('ctx', 'head'), may hold values from -8 to 8
- self_keys: bfloat16 [4096, 1024], P('ctx', 'head'), may hold values from -8 to 8
- self_values: bfloat16 [4096, 1024], P('ctx', 'head'), may hold values from -6 to 6
- cross_queries: bfloat16 [4096, 8192], P('ctx', 'head'), may hold values from -8 to 8
- image_keys: bfloat16 [32, 1601, 1024], P('ctx', None, 'head'), may hold values from -8 to 8
- image_values: bfloat16 [32, 1601, 1024], P('ctx', None, 'head'), may hold values from -6 to 6
- image_lists: int32 [32, 6], replicated, may hold values from 0 to 31, as said below
- image_counts: int32 [32], replicated, may hold values from 1 to 6, as said below
- doc_ids: int32 [4096], replicated, may hold values from 0 to 7, never falling along the last dimension, each value on 1 to 2176 neighbouring positions
Outputs:
- self_attended: bfloat16 [4096, 8192], P(('ctx', 'head'))
- cross_attended: bfloat16 [4096, 8192], P(('ctx', 'head'))
The draws below stay inside these ranges and needn't reach their ends.
Inputs may be any that keep to these rules, and one draw needn't show every extreme that they name: `image_lists`: the ids of one list are distinct; each image is the first entry of exactly one span's list; image i is held by index i of ctx. `image_counts`: some span uses all 6 entries.
All inputs are finite; a program needn't handle non-finite values.
Results may differ from the reference program's by a relative error of at most 0.024.
Values may be sent and summed in bfloat16 or wider, within the bound.
No kernel may reach another device: no remote copies, remote signals or barrier semaphores. Data moves between devices by JAX's collectives and lax.ppermute only.
A program may use at most 128 MiB of HBM per device.

```python
import math
import jax
import jax.numpy as jnp
import numpy as np
from jax import lax

H = 64
KVH = 8
HD = 128
TOK_DEV = 128
IMG_TOK = 1601
LIST = 6
DOCS = 8
TOKENS = 4096
SPANS = 32
NIMG = 32
DOC_MOST = 2176


def rough_base(key, shape, tag):
    return jax.random.truncated_normal(jax.random.fold_in(key, tag), -6.0, 6.0, shape, jnp.float32)


def drawn_queries(key, tag):
    values = rough_base(key, (TOKENS, H * HD), tag)
    return values.astype(jnp.bfloat16)


def draw_self_queries(key, part):
    return drawn_queries(key, 11)


def draw_cross_queries(key, part):
    return drawn_queries(key, 13)


def draw_self_keys(key, part):
    values = rough_base(key, (TOKENS, KVH * HD), 15)
    return values.astype(jnp.bfloat16)


def draw_image_keys(key, part):
    values = rough_base(key, (NIMG, IMG_TOK, KVH * HD), 17)
    return values.astype(jnp.bfloat16)


def draw_image_lists(key, part):
    leaders = jax.random.permutation(jax.random.fold_in(key, 31), NIMG).astype(jnp.int32)
    row_keys = jax.random.split(jax.random.fold_in(key, 32), SPANS)
    others = jax.vmap(lambda row_key: jax.random.permutation(row_key, NIMG - 1)[:LIST - 1])(row_keys).astype(jnp.int32)
    chosen = (leaders[:SPANS, None] + 1 + others) % NIMG
    return jnp.concatenate([leaders[:SPANS, None], chosen], axis=1).astype(jnp.int32)


def draw_image_counts(key, part):
    counts = jax.random.randint(jax.random.fold_in(key, 21), (SPANS,), 1, LIST + 1).astype(jnp.int32)
    picked = jax.random.randint(jax.random.fold_in(key, 22), (), 0, SPANS)
    return counts.at[picked].set(LIST).astype(jnp.int32)


def shard_levels(stream_key, dims, cuts, least, high):
    def one(dim, blocks):
        draws = jax.random.uniform(jax.random.fold_in(jax.random.fold_in(stream_key, 6), dim), (blocks,), jnp.float32, least / len(cuts), high / len(cuts))
        return jnp.repeat(jnp.exp(draws), dims[dim] // blocks).reshape((-1,) + (1,) * (len(dims) - dim - 1))

    gain = one(*cuts[0])
    for cut in cuts[1:]:
        gain = gain * one(*cut)
    return gain


def profile(count, total, reach, lean):
    portions = [(1 << 20) // math.isqrt(grade ** lean) + 1 for grade in range(2, count + 1)]
    rest, given = total - reach - (count - 1), [1] * (count - 1)
    while rest > 0:
        free = [i for i in range(count - 1) if given[i] < reach]
        whole, budget = sum([portions[i] for i in free]), rest
        for i in free:
            addition = min(reach - given[i], max(1, budget * portions[i] // whole), rest)
            given[i] = given[i] + addition
            rest = rest - addition
    return np.array([reach] + given)


def uneven_parts(key, number_of, total, bound, slope):
    if number_of == 2:
        one = jax.random.randint(key, (), max(1, total - bound), min(bound, total - 1) + 1)
        return jnp.stack([one, total - one])
    lengths = jnp.asarray(profile(number_of, total, bound, slope), jnp.int32)
    couples = (number_of - 1) // 2
    donor, sink = lengths[1:1 + 2 * couples:2], lengths[2:2 + 2 * couples:2]
    margin = jnp.minimum(donor - 1, bound - sink)
    shifted = jax.random.randint(jax.random.fold_in(key, 1), (couples,), 0, 1 << 20) % (margin + 1)
    lengths = lengths.at[1:1 + 2 * couples:2].set(donor - shifted).at[2:2 + 2 * couples:2].set(sink + shifted)
    return lengths[jax.random.permutation(jax.random.fold_in(key, 2), number_of)]


def noise(key, shape, spread, bound, cuts=(), held_as=jnp.bfloat16):
    values = spread * jax.random.normal(key, shape, jnp.float32)
    if cuts:
        values = values * shard_levels(key, shape, cuts, -0.22, 0.18)
    return jnp.clip(values, -bound, bound).astype(held_as)


def setup_inputs(seed: int = 0) -> dict:
    key_of = jax.random.split(jax.random.key(seed), 10)
    return {
        "self_queries": draw_self_queries(jax.random.fold_in(key_of[9], 71), 0),
        "self_keys": draw_self_keys(jax.random.fold_in(key_of[9], 71), 0),
        "self_values": noise(key_of[2], (TOKENS, KVH * HD), 1.0, 6.0, ((0, 32), (1, 8))),
        "cross_queries": draw_cross_queries(jax.random.fold_in(key_of[9], 71), 0),
        "image_keys": draw_image_keys(jax.random.fold_in(key_of[9], 71), 0),
        "image_values": noise(key_of[5], (NIMG, IMG_TOK, KVH * HD), 1.0, 6.0, ((0, 32), (2, 8))),
        "image_lists": draw_image_lists(jax.random.fold_in(key_of[9], 71), 0),
        "image_counts": draw_image_counts(jax.random.fold_in(key_of[9], 71), 0),
        "doc_ids": jnp.searchsorted(jnp.cumsum(uneven_parts(key_of[8], DOCS, TOKENS, DOC_MOST, 2)), jnp.arange(TOKENS), side="right").astype(jnp.int32),
    }


def reference(self_queries, self_keys, self_values, cross_queries, image_keys, image_values, image_lists, image_counts, doc_ids):
    score_scale = 1.0 / math.sqrt(HD)
    group_size = H // KVH
    positions = jnp.arange(TOKENS, dtype=jnp.int32)
    allowed = (positions[None, :] <= positions[:, None]) & (doc_ids[None, :] == doc_ids[:, None])
    query_heads = self_queries.reshape(TOKENS, H, HD).transpose(1, 0, 2)
    key_heads = self_keys.reshape(TOKENS, KVH, HD).transpose(1, 0, 2)
    value_heads = self_values.reshape(TOKENS, KVH, HD).transpose(1, 0, 2)

    def one_head(inputs):
        query_rows, head_id = inputs
        head_keys = key_heads[head_id // group_size]
        head_values = value_heads[head_id // group_size]
        scores = jnp.dot(query_rows, head_keys.T, preferred_element_type=jnp.float32) * score_scale
        scores = jnp.where(allowed, scores, jnp.float32(-1e+30))
        highest = lax.optimization_barrier(jnp.max(scores, axis=1, keepdims=True))
        weights = jnp.where(allowed, jnp.exp(scores - highest), jnp.float32(0.0))
        row_total = lax.optimization_barrier(jnp.sum(weights, axis=1, keepdims=True))
        output = jnp.dot(weights.astype(jnp.bfloat16), head_values, preferred_element_type=jnp.float32) / row_total
        return output.astype(jnp.bfloat16)
    self_heads = lax.map(one_head, (query_heads, jnp.arange(H, dtype=jnp.int32)))
    self_attended = self_heads.transpose(1, 0, 2).reshape(TOKENS, H * HD)

    def one_span(span_id):
        query_rows = lax.dynamic_slice_in_dim(cross_queries, span_id * TOK_DEV, TOK_DEV, 0)
        query_rows = query_rows.astype(jnp.float32).reshape(TOK_DEV, KVH, group_size, HD)
        outputs = []
        log_totals = []
        for slot in range(LIST):
            image_id = image_lists[span_id, slot]
            image_key = image_keys[image_id].astype(jnp.float32).reshape(IMG_TOK, KVH, HD)
            image_value = image_values[image_id].astype(jnp.float32).reshape(IMG_TOK, KVH, HD)
            scores = jnp.einsum('tkgd,skd->tkgs', query_rows, image_key, precision=lax.Precision.HIGHEST) * score_scale
            highest = lax.optimization_barrier(jnp.max(scores, axis=3, keepdims=True))
            weights = jnp.exp(scores - highest)
            row_total = lax.optimization_barrier(jnp.sum(weights, axis=3))
            rounded = lax.optimization_barrier(weights.astype(jnp.bfloat16)).astype(jnp.float32)
            output = jnp.einsum('tkgs,skd->tkgd', rounded, image_value, precision=lax.Precision.HIGHEST) / row_total[..., None]
            outputs.append(output.astype(jnp.bfloat16))
            log_total = highest[..., 0] + jnp.log(row_total)
            log_totals.append(jnp.where(slot < image_counts[span_id], log_total, jnp.float32(-1e+30)))
        stacked = jnp.stack(log_totals)
        highest_level = lax.optimization_barrier(jnp.max(stacked, axis=0))
        shares = jnp.exp(stacked - highest_level[None])
        shares = shares / lax.optimization_barrier(jnp.sum(shares, axis=0))[None]
        blended = jnp.zeros((TOK_DEV, KVH, group_size, HD), jnp.float32)
        for slot in range(LIST):
            blended = blended + shares[slot][..., None] * outputs[slot].astype(jnp.float32)
        return blended.astype(jnp.bfloat16).reshape(TOK_DEV, H * HD)
    cross_spans = lax.map(one_span, jnp.arange(SPANS, dtype=jnp.int32))
    cross_attended = cross_spans.reshape(TOKENS, H * HD)
    return (self_attended, cross_attended)
```

```python
import functools
import math

import jax
import jax.numpy as jnp
from jax import lax
from jax.experimental import pallas as pl
from jax.experimental.pallas import tpu as pltpu
from jax.sharding import PartitionSpec as P

HD = 128
LIST = 6
GROUP = 8
ROWS = 128
NX = 4
NZ = 8
WIDE = GROUP * HD
HALF = WIDE // 2
PACK = WIDE + HD
HALF_PACK = HALF + HD
LOW = -1e30
START = -1e29
SCALE2 = math.log2(math.e) / math.sqrt(HD)
MIB = 1024 * 1024
F32 = jnp.float32
BF16 = jnp.bfloat16

Z_GROUPS = [[NX * z + x for z in range(NZ)] for x in range(NX)]


def moved(array, dz, dx):
    pairs = [
        (NX * z + x, NX * ((z + dz) % NZ) + (x + dx) % NX) for z in range(NZ) for x in range(NX)
    ]
    return lax.ppermute(array, "ctx", pairs)


def nt(a, b):
    return lax.dot_general(a, b, (((1,), (1,)), ((), ())), preferred_element_type=F32)


def nn(a, b):
    return lax.dot_general(a, b, (((1,), (0,)), ((), ())), preferred_element_type=F32)


def absorb(query_rows, keys, values, top_ref, total_ref, at, bias=None):
    rows = query_rows.shape[0]
    scores = nt(query_rows, keys) * SCALE2
    if bias is not None:
        scores = scores + bias
    block = pl.ds(at, rows)
    old = top_ref[block, :]
    new = jnp.maximum(old, jnp.max(scores, axis=1, keepdims=True))
    weights = jnp.exp2(scores - new[:, :1]).astype(BF16)
    wide_values = jnp.concatenate([values, jnp.ones_like(values)], axis=1)
    fade = jnp.exp2(old - new)
    total_ref[block, :] = total_ref[block, :] * jnp.concatenate([fade, fade], axis=1) + nn(
        weights, wide_values
    )
    top_ref[block, :] = new


def head_cols(h):
    return slice(h * HD, (h + 1) * HD)


def lse_lanes(levels, heads):
    lane = lax.broadcasted_iota(jnp.int32, (ROWS, HD), 1)
    both = jnp.zeros((ROWS, HD), F32)
    for h, level in zip(heads, levels):
        both = jnp.where(lane % GROUP == h, level, both)
    high = both.astype(BF16).astype(F32)
    middle = (both - high).astype(BF16).astype(F32)
    low = both - high - middle
    picked = jnp.where(lane < GROUP, high, jnp.where(lane < 2 * GROUP, middle, low))
    return jnp.where(lane < 3 * GROUP, picked, 0.0).astype(BF16)


def lse_of(lanes, h):
    return lanes[:, h : h + 1] + lanes[:, GROUP + h : GROUP + h + 1] + lanes[:, 2 * GROUP + h : 2 * GROUP + h + 1]


def image_kernel(shifts, halves, place, lists, counts, *refs):
    query_ref = refs[0]
    key_refs, value_refs = refs[1 : 1 + NX], refs[1 + NX : 1 + 2 * NX]
    outs = refs[1 + 2 * NX : -6]
    key_buf, value_buf, top_ref, total_ref, key_sem, value_sem = refs[-6:]
    z, x = place[0], place[1]
    step = pl.program_id(0)
    shift = jnp.int32(shifts[0])
    for n, value in enumerate(shifts):
        shift = jnp.where(step == n, value, shift)
    span = NX * lax.rem(z + shift, NZ) + x
    top_ref[...] = jnp.full_like(top_ref, START)
    total_ref[...] = jnp.zeros_like(total_ref)
    for back in range(NX):
        image = NX * z + lax.rem(x + NX - back, NX)
        wanted = False
        for j in range(LIST):
            wanted = jnp.logical_or(
                wanted, jnp.logical_and(j < counts[span], lists[span, j] == image)
            )

        @pl.when(wanted)
        def _(back=back):
            key_copy = pltpu.make_async_copy(key_refs[back], key_buf, key_sem)
            value_copy = pltpu.make_async_copy(value_refs[back], value_buf, value_sem)
            key_copy.start()
            value_copy.start()
            key_copy.wait()
            value_copy.wait()
            for pair in range(GROUP // 2):
                rows = jnp.concatenate(
                    [query_ref[0, :, head_cols(2 * pair + k)] for k in range(2)], axis=0
                )
                absorb(rows, key_buf[0], value_buf[0], top_ref, total_ref, 2 * pair * ROWS)

    levels, parts = [], []
    for h in range(GROUP):
        block = pl.ds(h * ROWS, ROWS)
        row_total = total_ref[block, HD:]
        used = row_total > 0.0
        safe = jnp.where(used, row_total, 1.0)
        parts.append((total_ref[block, :HD] / safe).astype(BF16))
        levels.append(jnp.where(used, top_ref[block, :] + jnp.log2(safe), LOW))
    lanes = lse_lanes(levels, range(GROUP))
    if halves:
        first, second = outs
        for h in range(GROUP // 2):
            first[0, :, head_cols(h)] = parts[h]
            second[0, :, head_cols(h)] = parts[GROUP // 2 + h]
        first[0, :, HALF:] = lanes
        second[0, :, HALF:] = lanes
    else:
        (out,) = outs
        for h in range(GROUP):
            out[0, :, head_cols(h)] = parts[h]
        out[0, :, WIDE:] = lanes


def image_parts(place, lists, counts, queries, keys, values, shifts, halves=False):
    def query_block(n, place, lists, counts):
        shift = jnp.int32(shifts[0])
        for k, value in enumerate(shifts):
            shift = jnp.where(n == k, value, shift)
        return (lax.rem(place[0] + shift, NZ), 0, 0)

    widths = [HALF_PACK, HALF_PACK] if halves else [PACK]
    any_spec = pl.BlockSpec(memory_space=pl.ANY)
    tokens = keys[0].shape[1]
    out = pl.pallas_call(
        functools.partial(image_kernel, shifts, halves),
        grid_spec=pltpu.PrefetchScalarGridSpec(
            num_scalar_prefetch=3,
            grid=(len(shifts),),
            in_specs=[pl.BlockSpec((1, ROWS, WIDE), query_block)] + [any_spec] * (2 * NX),
            out_specs=[
                pl.BlockSpec((1, ROWS, w), lambda n, place, lists, counts: (n, 0, 0))
                for w in widths
            ],
            scratch_shapes=[
                pltpu.VMEM((1, tokens, HD), BF16),
                pltpu.VMEM((1, tokens, HD), BF16),
                pltpu.VMEM((GROUP * ROWS, HD), F32),
                pltpu.VMEM((GROUP * ROWS, 2 * HD), F32),
                pltpu.SemaphoreType.DMA,
                pltpu.SemaphoreType.DMA,
            ],
        ),
        out_shape=[jax.ShapeDtypeStruct((len(shifts), ROWS, w), BF16) for w in widths],
        compiler_params=pltpu.CompilerParams(vmem_limit_bytes=40 * MIB),
        cost_estimate=pl.CostEstimate(
            flops=len(shifts) * 10**9, bytes_accessed=len(shifts) * 2 * 10**6, transcendentals=0
        ),
        name="image_parts_" + "_".join(str(s) for s in shifts),
    )(place, lists, counts, queries, *keys, *values)
    return out


def merged(a, level_a, b, level_b):
    top = jnp.maximum(level_a, level_b)
    share_a, share_b = jnp.exp2(level_a - top), jnp.exp2(level_b - top)
    total = share_a + share_b
    return (share_a * a + share_b * b) / total, top + jnp.log2(total)


def first_merge_kernel(plus_in, minus_in, local_ref, plus_out, minus_out):
    for arrived, side, out, low in (
        (plus_in, 0, plus_out, 0),
        (minus_in, 1, minus_out, GROUP // 2),
    ):
        lanes, own_lanes = arrived[0, :, HALF:].astype(F32), local_ref[side, :, WIDE:].astype(F32)
        levels = []
        for h in range(GROUP):
            own, own_level = local_ref[side, :, head_cols(h)], lse_of(own_lanes, h)
            if low <= h < low + GROUP // 2:
                part, level = merged(
                    arrived[0, :, head_cols(h - low)].astype(F32),
                    lse_of(lanes, h),
                    own.astype(F32),
                    own_level,
                )
                out[0, :, head_cols(h)] = part.astype(BF16)
                levels.append(level)
            else:
                out[0, :, head_cols(h)] = own
                levels.append(own_level)
        out[0, :, WIDE:] = lse_lanes(levels, range(GROUP))


def merge_kernel(plus_in, minus_in, local_ref, plus_out, minus_out):
    for arrived, side, out in ((plus_in, 0, plus_out), (minus_in, 1, minus_out)):
        lanes, own_lanes = arrived[0, :, WIDE:].astype(F32), local_ref[side, :, WIDE:].astype(F32)
        levels = []
        for h in range(GROUP):
            part, level = merged(
                arrived[0, :, head_cols(h)].astype(F32),
                lse_of(lanes, h),
                local_ref[side, :, head_cols(h)].astype(F32),
                lse_of(own_lanes, h),
            )
            out[0, :, head_cols(h)] = part.astype(BF16)
            levels.append(level)
        out[0, :, WIDE:] = lse_lanes(levels, range(GROUP))


def last_merge_kernel(plus_in, minus_in, local_ref, out):
    lanes = [r[0, :, WIDE:].astype(F32) for r in (plus_in, minus_in, local_ref)]
    for h in range(GROUP):
        part, level = merged(
            plus_in[0, :, head_cols(h)].astype(F32),
            lse_of(lanes[0], h),
            minus_in[0, :, head_cols(h)].astype(F32),
            lse_of(lanes[1], h),
        )
        part, _ = merged(part, level, local_ref[0, :, head_cols(h)].astype(F32), lse_of(lanes[2], h))
        out[:, head_cols(h)] = part.astype(BF16)


def small_call(kernel, out_shape, name, *args):
    return pl.pallas_call(
        kernel,
        out_shape=out_shape,
        compiler_params=pltpu.CompilerParams(vmem_limit_bytes=24 * MIB),
        cost_estimate=pl.CostEstimate(flops=10**7, bytes_accessed=2 * 10**6, transcendentals=0),
        name=name,
    )(*args)


def self_kernel(place, starts_ref, query_ref, *refs):
    kv_refs, out_ref, top_ref, total_ref = refs[:NX], refs[NX], refs[NX + 1], refs[NX + 2]
    z, x, earliest = place[0], place[1], place[2]
    first = (NX * z + x) * ROWS
    top_ref[...] = jnp.full_like(top_ref, START)
    total_ref[...] = jnp.zeros_like(total_ref)
    row_pos = first + lax.broadcasted_iota(jnp.int32, (ROWS, 2 * ROWS), 0)
    key_step = lax.broadcasted_iota(jnp.int32, (ROWS, 2 * ROWS), 1)
    key_off = jnp.where(key_step >= ROWS, key_step + (NX - 1) * ROWS, key_step)
    starts = starts_ref[...]
    low = earliest // (2 * NX * ROWS)
    for back in range(NX):
        column = lax.rem(x + NX - back, NX)

        def body(p, carry, back=back, column=column):
            key_pos = (2 * NX * p + column) * ROWS + key_off
            seen = jnp.logical_and(key_pos <= row_pos, key_pos >= starts)
            bias = jnp.where(seen, 0.0, LOW)
            bias = jnp.concatenate([bias, bias], axis=0)
            keys = jnp.concatenate([kv_refs[back][2 * p + k, :, :HD] for k in range(2)], axis=0)
            values = jnp.concatenate([kv_refs[back][2 * p + k, :, HD:] for k in range(2)], axis=0)
            for pair in range(GROUP // 2):
                rows = jnp.concatenate(
                    [query_ref[:, head_cols(2 * pair + k)] for k in range(2)], axis=0
                )
                absorb(rows, keys, values, top_ref, total_ref, 2 * pair * ROWS, bias)
            return carry

        lax.fori_loop(low, z // 2 + 1, body, 0)
    for h in range(GROUP):
        block = pl.ds(h * ROWS, ROWS)
        out_ref[:, head_cols(h)] = (total_ref[block, :HD] / total_ref[block, HD:]).astype(BF16)


def self_attention(place, starts, queries, kv):
    vmem = pl.BlockSpec(memory_space=pltpu.VMEM)
    return pl.pallas_call(
        self_kernel,
        grid_spec=pltpu.PrefetchScalarGridSpec(
            num_scalar_prefetch=1,
            grid=(),
            in_specs=[vmem] * (2 + NX),
            out_specs=vmem,
            scratch_shapes=[
                pltpu.VMEM((GROUP * ROWS, HD), F32),
                pltpu.VMEM((GROUP * ROWS, 2 * HD), F32),
            ],
        ),
        out_shape=jax.ShapeDtypeStruct((ROWS, WIDE), BF16),
        compiler_params=pltpu.CompilerParams(vmem_limit_bytes=32 * MIB),
        cost_estimate=pl.CostEstimate(
            flops=2 * 10**9, bytes_accessed=4 * 10**6, transcendentals=0
        ),
        name="self_attention",
    )(place, starts, queries, *kv)


def on_device(
    self_queries,
    self_keys,
    self_values,
    cross_queries,
    image_keys,
    image_values,
    image_lists,
    image_counts,
    doc_ids,
):
    span = lax.axis_index("ctx")
    own_docs = lax.dynamic_slice_in_dim(doc_ids, span * ROWS, ROWS)
    starts = jnp.sum((doc_ids[None, :] < own_docs[:, None]).astype(jnp.int32), axis=1)
    place = jnp.stack([span // NX, span % NX, starts[0]]).astype(jnp.int32)
    starts = jnp.broadcast_to(starts[:, None], (ROWS, 2 * ROWS))

    sent = jnp.concatenate([cross_queries, self_keys, self_values], axis=1)[None]
    gathered = lax.all_gather(sent, "ctx", axis=0, tiled=True, axis_index_groups=Z_GROUPS)
    keys = [image_keys] + [moved(image_keys, 0, k) for k in (1, 2, 3)]
    values = [image_values] + [moved(image_values, 0, k) for k in (1, 2, 3)]

    own_kv = gathered[:, :, WIDE:]
    kv = [own_kv] + [moved(own_kv, 0, k) for k in (1, 2, 3)]

    parts = functools.partial(
        image_parts, place, image_lists, image_counts, gathered, keys, values
    )
    full = jax.ShapeDtypeStruct((1, ROWS, PACK), BF16)
    plus, minus = parts((4,), halves=True)
    plus, minus = moved(plus, 1, 0), moved(minus, -1, 0)
    for distance in (3, 2, 1):
        (local,) = parts((distance, NZ - distance))
        kernel = first_merge_kernel if distance == 3 else merge_kernel
        plus, minus = small_call(kernel, (full, full), f"merge_{distance}", plus, minus, local)
        plus, minus = moved(plus, 1, 0), moved(minus, -1, 0)
    (local,) = parts((0,))
    cross_out = small_call(
        last_merge_kernel,
        jax.ShapeDtypeStruct((ROWS, WIDE), BF16),
        "merge_0",
        plus,
        minus,
        local,
    )
    self_out = self_attention(place, starts, self_queries, kv)
    return tuple(
        lax.all_to_all(out, "head", split_axis=0, concat_axis=1, tiled=True)
        for out in (self_out, cross_out)
    )


def solution(mesh):
    in_specs = (
        P("ctx", "head"),
        P("ctx", "head"),
        P("ctx", "head"),
        P("ctx", "head"),
        P("ctx", None, "head"),
        P("ctx", None, "head"),
        P(),
        P(),
        P(),
    )
    out_specs = (P(("ctx", "head"), None), P(("ctx", "head"), None))
    return jax.shard_map(
        on_device, mesh=mesh, in_specs=in_specs, out_specs=out_specs, check_vma=False
    )
```

```python
import functools
import math

import jax
import jax.numpy as jnp
from jax import lax
from jax.experimental import pallas as pl
from jax.experimental.pallas import tpu as pltpu
from jax.sharding import PartitionSpec as P

HD = 128
LIST = 6
GROUP = 8
ROWS = 128
NX = 4
NZ = 8
WIDE = GROUP * HD
HALF = WIDE // 2
PACK = WIDE + HD
HALF_PACK = HALF + HD
LOW = -1e30
START = -1e29
SCALE2 = math.log2(math.e) / math.sqrt(HD)
MIB = 1024 * 1024
F32 = jnp.float32
BF16 = jnp.bfloat16

def moved(array, dz, dx):
    pairs = [
        (NX * z + x, NX * ((z + dz) % NZ) + (x + dx) % NX) for z in range(NZ) for x in range(NX)
    ]
    return lax.ppermute(array, "ctx", pairs)


def nt(a, b):
    return lax.dot_general(a, b, (((1,), (1,)), ((), ())), preferred_element_type=F32)


def nn(a, b):
    return lax.dot_general(a, b, (((1,), (0,)), ((), ())), preferred_element_type=F32)


def attend(query_blocks, keys, values, top_ref, total_ref, bias=None):
    wide_values = jnp.concatenate([values, jnp.ones_like(values)], axis=1)
    rows = query_blocks[0].shape[0]
    ahead = nt(query_blocks[0], keys)
    for n in range(len(query_blocks)):
        scores = ahead
        if n + 1 < len(query_blocks):
            ahead = nt(query_blocks[n + 1], keys)
        block = slice(n * rows, (n + 1) * rows)
        if bias is not None:
            scores = scores + bias
        old = top_ref[block, :]
        new = jnp.maximum(old, jnp.max(scores, axis=1, keepdims=True) * SCALE2)
        weights = jnp.exp2(scores * SCALE2 - new[:, :1]).astype(BF16)
        fade = jnp.exp2(old - new)
        total_ref[block, :] = total_ref[block, :] * jnp.concatenate([fade, fade], axis=1) + nn(
            weights, wide_values
        )
        top_ref[block, :] = new


def head_cols(h):
    return slice(h * HD, (h + 1) * HD)


def lse_lanes(levels, heads):
    lane = lax.broadcasted_iota(jnp.int32, (ROWS, HD), 1)
    both = jnp.zeros((ROWS, HD), F32)
    for h, level in zip(heads, levels):
        both = jnp.where(lane % GROUP == h, level, both)
    high = both.astype(BF16).astype(F32)
    middle = (both - high).astype(BF16).astype(F32)
    low = both - high - middle
    picked = jnp.where(lane < GROUP, high, jnp.where(lane < 2 * GROUP, middle, low))
    return jnp.where(lane < 3 * GROUP, picked, 0.0).astype(BF16)


def lse_of(lanes, h):
    return lanes[:, h : h + 1] + lanes[:, GROUP + h : GROUP + h + 1] + lanes[:, 2 * GROUP + h : 2 * GROUP + h + 1]


def image_kernel(shifts, halves, place, lists, counts, *refs):
    number = len(shifts)
    query_refs = refs[: 2 * number]
    key_refs, value_refs = refs[2 * number : 2 * number + NX], refs[2 * number + NX : 2 * number + 2 * NX]
    outs = refs[-11:-9] if halves else refs[-10:-9]
    key_buf, value_buf, row_buf, top_ref, total_ref, work, amount, key_sem, value_sem = refs[-9:]
    z, x = place[0], place[1]
    amount[0] = 0
    for n, shift in enumerate(shifts):
        span = NX * lax.rem(z + shift, NZ) + x
        for back in range(NX):
            image = NX * z + lax.rem(x + NX - back, NX)
            wanted = False
            for j in range(LIST):
                wanted = jnp.logical_or(
                    wanted, jnp.logical_and(j < counts[span], lists[span, j] == image)
                )

            @pl.when(wanted)
            def _(n=n, back=back):
                at = amount[0]
                work[at] = n * NX + back
                amount[0] = at + 1

    def copies(back, slot):
        return (
            pltpu.make_async_copy(key_refs[back], key_buf.at[pl.ds(slot, 1)], key_sem.at[slot]),
            pltpu.make_async_copy(
                value_refs[back], value_buf.at[pl.ds(slot, 1)], value_sem.at[slot]
            ),
        )

    def fetch(entry, slot):
        for back in range(NX):

            @pl.when(lax.rem(entry, NX) == back)
            def _(back=back):
                for copy in copies(back, slot):
                    copy.start()

    @pl.when(amount[0] > 0)
    def _():
        fetch(work[0], 0)

    for n in range(number):
        for h in range(GROUP):
            side, at = divmod(h, GROUP // 2)
            row_buf[n, h * ROWS : (h + 1) * ROWS, :] = query_refs[2 * n + side][:, head_cols(at)]
    top_ref[...] = jnp.full_like(top_ref, START)
    total_ref[...] = jnp.zeros_like(total_ref)

    def visit(i, carry):
        slot = lax.rem(i, 2)
        entry = work[i]

        @pl.when(i + 1 < amount[0])
        def _():
            fetch(work[i + 1], 1 - slot)

        for copy in copies(0, slot):
            copy.wait()
        n = entry // NX
        half = GROUP * ROWS // 2
        blocks = [row_buf[n, k * half : (k + 1) * half, :] for k in range(2)]
        attend(blocks, key_buf[slot], value_buf[slot], top_ref.at[n], total_ref.at[n])
        return carry

    lax.fori_loop(0, amount[0], visit, 0)

    for n in range(number):
        levels, parts = [], []
        for h in range(GROUP):
            block = slice(h * ROWS, (h + 1) * ROWS)
            row_total = total_ref[n, block, HD:]
            used = row_total > 0.0
            safe = jnp.where(used, row_total, 1.0)
            parts.append((total_ref[n, block, :HD] / safe).astype(BF16))
            levels.append(jnp.where(used, top_ref[n, block, :] + jnp.log2(safe), LOW))
        lanes = lse_lanes(levels, range(GROUP))
        if halves:
            first, second = outs
            for h in range(GROUP // 2):
                first[n, :, head_cols(h)] = parts[h]
                second[n, :, head_cols(h)] = parts[GROUP // 2 + h]
            first[n, :, HALF:] = lanes
            second[n, :, HALF:] = lanes
        else:
            (out,) = outs
            for h in range(GROUP):
                out[n, :, head_cols(h)] = parts[h]
            out[n, :, WIDE:] = lanes


def image_parts(place, lists, counts, keys, values, shifts, queries, earlier, halves=False):
    widths = [HALF_PACK, HALF_PACK] if halves else [PACK]
    number = len(shifts)
    tokens = keys[0].shape[1]
    query_specs = [
        pl.BlockSpec((ROWS, HALF), lambda i, *_, at=at: (0, at)) for _, at in queries
    ]
    return pl.pallas_call(
        functools.partial(image_kernel, shifts, halves),
        grid_spec=pltpu.PrefetchScalarGridSpec(
            num_scalar_prefetch=3,
            grid=(1,),
            in_specs=query_specs
            + [pl.BlockSpec(memory_space=pltpu.HBM)] * (2 * NX)
            + [pl.BlockSpec(memory_space=pl.ANY)] * len(earlier),
            out_specs=[pl.BlockSpec((number, ROWS, w), lambda i, *_: (0, 0, 0)) for w in widths],
            scratch_shapes=[
                pltpu.VMEM((2, tokens, HD), BF16),
                pltpu.VMEM((2, tokens, HD), BF16),
                pltpu.VMEM((number, GROUP * ROWS, HD), BF16),
                pltpu.VMEM((number, GROUP * ROWS, HD), F32),
                pltpu.VMEM((number, GROUP * ROWS, 2 * HD), F32),
                pltpu.SMEM((2 * NX,), jnp.int32),
                pltpu.SMEM((1,), jnp.int32),
                pltpu.SemaphoreType.DMA((2,)),
                pltpu.SemaphoreType.DMA((2,)),
            ],
        ),
        out_shape=[jax.ShapeDtypeStruct((number, ROWS, w), BF16) for w in widths],
        compiler_params=pltpu.CompilerParams(vmem_limit_bytes=40 * MIB),
        cost_estimate=pl.CostEstimate(
            flops=number * 10**9, bytes_accessed=number * 2 * 10**6, transcendentals=0
        ),
        name="image_parts_" + "_".join(str(s) for s in shifts),
    )(place, lists, counts, *[a for a, _ in queries], *keys, *values, *earlier)


def merged(a, level_a, b, level_b):
    top = jnp.maximum(level_a, level_b)
    share_a, share_b = jnp.exp2(level_a - top), jnp.exp2(level_b - top)
    total = share_a + share_b
    return (share_a * a + share_b * b) / total, top + jnp.log2(total)


def first_merge_kernel(plus_in, minus_in, local_ref, plus_out, minus_out):
    for arrived, side, out, low in (
        (plus_in, 0, plus_out, 0),
        (minus_in, 1, minus_out, GROUP // 2),
    ):
        lanes, own_lanes = arrived[0, :, HALF:].astype(F32), local_ref[side, :, WIDE:].astype(F32)
        levels = []
        for h in range(GROUP):
            own, own_level = local_ref[side, :, head_cols(h)], lse_of(own_lanes, h)
            if low <= h < low + GROUP // 2:
                part, level = merged(
                    arrived[0, :, head_cols(h - low)].astype(F32),
                    lse_of(lanes, h),
                    own.astype(F32),
                    own_level,
                )
                out[0, :, head_cols(h)] = part.astype(BF16)
                levels.append(level)
            else:
                out[0, :, head_cols(h)] = own
                levels.append(own_level)
        out[0, :, WIDE:] = lse_lanes(levels, range(GROUP))


def merge_kernel(plus_in, minus_in, local_ref, plus_out, minus_out):
    for arrived, side, out in ((plus_in, 0, plus_out), (minus_in, 1, minus_out)):
        lanes, own_lanes = arrived[0, :, WIDE:].astype(F32), local_ref[side, :, WIDE:].astype(F32)
        levels = []
        for h in range(GROUP):
            part, level = merged(
                arrived[0, :, head_cols(h)].astype(F32),
                lse_of(lanes, h),
                local_ref[side, :, head_cols(h)].astype(F32),
                lse_of(own_lanes, h),
            )
            out[0, :, head_cols(h)] = part.astype(BF16)
            levels.append(level)
        out[0, :, WIDE:] = lse_lanes(levels, range(GROUP))


def last_merge_kernel(plus_in, minus_in, local_ref, self_ref, out):
    out[:, :WIDE] = self_ref[...]
    lanes = [r[0, :, WIDE:].astype(F32) for r in (plus_in, minus_in, local_ref)]
    for h in range(GROUP):
        part, level = merged(
            plus_in[0, :, head_cols(h)].astype(F32),
            lse_of(lanes[0], h),
            minus_in[0, :, head_cols(h)].astype(F32),
            lse_of(lanes[1], h),
        )
        part, _ = merged(part, level, local_ref[0, :, head_cols(h)].astype(F32), lse_of(lanes[2], h))
        out[:, head_cols(GROUP + h)] = part.astype(BF16)


def small_call(kernel, out_shape, name, *args):
    return pl.pallas_call(
        kernel,
        out_shape=out_shape,
        compiler_params=pltpu.CompilerParams(vmem_limit_bytes=24 * MIB),
        cost_estimate=pl.CostEstimate(flops=10**7, bytes_accessed=2 * 10**6, transcendentals=0),
        name=name,
    )(*args)


def self_kernel(place, starts_ref, query_ref, *refs):
    kv_refs, (out_ref, top_ref, total_ref) = refs[:NX], refs[-3:]
    z, x, earliest = place[0], place[1], place[2]
    first = (NX * z + x) * ROWS
    top_ref[...] = jnp.full_like(top_ref, START)
    total_ref[...] = jnp.zeros_like(total_ref)
    row_pos = first + lax.broadcasted_iota(jnp.int32, (ROWS, 2 * ROWS), 0)
    key_step = lax.broadcasted_iota(jnp.int32, (ROWS, 2 * ROWS), 1)
    key_off = jnp.where(key_step >= ROWS, key_step - (NX + 1) * ROWS, key_step)
    starts = starts_ref[...]
    chunks = (z - earliest // (NX * ROWS)) // 2 + 1
    blocks = [
        jnp.concatenate([query_ref[:, head_cols(2 * n + k)] for k in range(2)], axis=0)
        for n in range(GROUP // 2)
    ]
    for back in range(NX):
        column = lax.rem(x + NX - back, NX)

        def body(p, carry, back=back, column=column):
            key_pos = (NX * (z - 2 * p) + column) * ROWS + key_off
            seen = jnp.logical_and(key_pos <= row_pos, key_pos >= starts)
            bias = jnp.where(seen, 0.0, LOW)
            bias = jnp.concatenate([bias, bias], axis=0)
            keys = jnp.concatenate([kv_refs[back][2 * p + k, :, :HD] for k in range(2)], axis=0)
            values = jnp.concatenate([kv_refs[back][2 * p + k, :, HD:] for k in range(2)], axis=0)
            attend(blocks, keys, values, top_ref, total_ref, bias)
            return carry

        lax.fori_loop(0, chunks, body, 0)
    for h in range(GROUP):
        block = pl.ds(h * ROWS, ROWS)
        out_ref[:, head_cols(h)] = (total_ref[block, :HD] / total_ref[block, HD:]).astype(BF16)


def self_attention(place, starts, queries, kv, earlier):
    vmem = pl.BlockSpec(memory_space=pltpu.VMEM)
    return pl.pallas_call(
        self_kernel,
        grid_spec=pltpu.PrefetchScalarGridSpec(
            num_scalar_prefetch=1,
            grid=(),
            in_specs=[vmem] * (2 + NX) + [pl.BlockSpec(memory_space=pl.ANY)],
            out_specs=vmem,
            scratch_shapes=[
                pltpu.VMEM((GROUP * ROWS, HD), F32),
                pltpu.VMEM((GROUP * ROWS, 2 * HD), F32),
            ],
        ),
        out_shape=jax.ShapeDtypeStruct((ROWS, WIDE), BF16),
        compiler_params=pltpu.CompilerParams(vmem_limit_bytes=32 * MIB),
        cost_estimate=pl.CostEstimate(
            flops=2 * 10**9, bytes_accessed=4 * 10**6, transcendentals=0
        ),
        name="self_attention",
    )(place, starts, queries, *kv, earlier)


def on_device(
    self_queries,
    self_keys,
    self_values,
    cross_queries,
    image_keys,
    image_values,
    image_lists,
    image_counts,
    doc_ids,
):
    span = lax.axis_index("ctx")
    own_docs = lax.dynamic_slice_in_dim(doc_ids, span * ROWS, ROWS)
    starts = jnp.sum((doc_ids[None, :] < own_docs[:, None]).astype(jnp.int32), axis=1)
    place = jnp.stack([span // NX, span % NX, starts[0]]).astype(jnp.int32)
    starts = jnp.broadcast_to(starts[:, None], (ROWS, 2 * ROWS))

    keys, values = [image_keys] + [None] * 3, [image_values] + [None] * 3
    for back, shift in ((1, 1), (3, -1)):
        keys[back] = moved(image_keys, 0, shift)
        values[back] = moved(image_values, 0, shift)
    before, after = [cross_queries], [cross_queries]
    for _ in range(3):
        before.append(moved(before[-1], 1, 0))
        after.append(moved(after[-1], -1, 0))
    far_first = moved(before[3][:, :HALF], 1, 0)
    far_second = moved(after[3][:, HALF:], -1, 0)
    keys[2], values[2] = moved(keys[1], 0, 1), moved(values[3], 0, -1)

    span_kv = jnp.concatenate([self_keys, self_values], axis=1)
    own_kv = jnp.stack([span_kv] + [moved(span_kv, k, 0) for k in (1, 2, 3, 4, -3)])
    kv = [own_kv] + [moved(own_kv, 0, k) for k in (1, 2, 3)]

    parts = functools.partial(image_parts, place, image_lists, image_counts, keys, values)
    full = jax.ShapeDtypeStruct((1, ROWS, PACK), BF16)
    plus, minus = parts((4,), [(far_first, 0), (far_second, 0)], [], halves=True)
    last = plus
    plus, minus = moved(plus, 1, 0), moved(minus, -1, 0)
    for distance in (3, 2, 1):
        (local,) = parts(
            (distance, NZ - distance),
            [(block[distance], side) for block in (after, before) for side in (0, 1)],
            [last],
        )
        kernel = first_merge_kernel if distance == 3 else merge_kernel
        last, other = small_call(
            kernel, (full, full), f"merge_{distance}", plus, minus, local
        )
        plus, minus = moved(last, 1, 0), moved(other, -1, 0)
    (local,) = parts((0,), [(cross_queries, 0), (cross_queries, 1)], [last])
    self_out = self_attention(place, starts, self_queries, kv, local)
    both = small_call(
        last_merge_kernel,
        jax.ShapeDtypeStruct((ROWS, 2 * WIDE), BF16),
        "merge_0",
        plus,
        minus,
        local,
        self_out,
    )
    back = lax.all_to_all(
        both.reshape(GROUP, ROWS // GROUP, 2 * WIDE), "head", split_axis=0, concat_axis=0
    )
    return tuple(
        jnp.swapaxes(back[:, :, k * WIDE : (k + 1) * WIDE], 0, 1).reshape(
            ROWS // GROUP, GROUP * WIDE
        )
        for k in range(2)
    )


def solution(mesh):
    in_specs = (
        P("ctx", "head"),
        P("ctx", "head"),
        P("ctx", "head"),
        P("ctx", "head"),
        P("ctx", None, "head"),
        P("ctx", None, "head"),
        P(),
        P(),
        P(),
    )
    out_specs = (P(("ctx", "head"), None), P(("ctx", "head"), None))
    return jax.shard_map(
        on_device, mesh=mesh, in_specs=in_specs, out_specs=out_specs, check_vma=False
    )
```

```python
import functools
import math

import jax
import jax.numpy as jnp
from jax import lax
from jax.experimental import pallas as pl
from jax.experimental.pallas import tpu as pltpu
from jax.sharding import PartitionSpec as P

HD = 128
LIST = 6
GROUP = 8
ROWS = 128
NX = 4
NZ = 8
WIDE = GROUP * HD
HALF = WIDE // 2
PACK = WIDE + HD
HALF_PACK = HALF + HD
KV_ROWS = 6
LOW = -1e30
START = -1e29
SCALE2 = math.log2(math.e) / math.sqrt(HD)
MIB = 1024 * 1024
F32 = jnp.float32
BF16 = jnp.bfloat16

def moved(array, dz, dx):
    pairs = [
        (NX * z + x, NX * ((z + dz) % NZ) + (x + dx) % NX) for z in range(NZ) for x in range(NX)
    ]
    return lax.ppermute(array, "ctx", pairs)


def nt(a, b):
    return lax.dot_general(a, b, (((1,), (1,)), ((), ())), preferred_element_type=F32)


def nn(a, b):
    return lax.dot_general(a, b, (((1,), (0,)), ((), ())), preferred_element_type=F32)


def attend(query_blocks, keys, values, top_ref, total_ref, bias=None):
    wide_values = jnp.concatenate([values, jnp.ones_like(values)], axis=1)
    rows = query_blocks[0].shape[0]
    ahead = nt(query_blocks[0], keys)
    for n in range(len(query_blocks)):
        scores = ahead
        if n + 1 < len(query_blocks):
            ahead = nt(query_blocks[n + 1], keys)
        block = slice(n * rows, (n + 1) * rows)
        if bias is not None:
            scores = scores + bias
        old = top_ref[block, :]
        new = jnp.maximum(old, jnp.max(scores, axis=1, keepdims=True) * SCALE2)
        weights = jnp.exp2(scores * SCALE2 - new[:, :1]).astype(BF16)
        fade = jnp.exp2(old - new)
        total_ref[block, :] = total_ref[block, :] * jnp.concatenate([fade, fade], axis=1) + nn(
            weights, wide_values
        )
        top_ref[block, :] = new


def head_cols(h):
    return slice(h * HD, (h + 1) * HD)


def lse_lanes(levels, heads):
    lane = lax.broadcasted_iota(jnp.int32, (ROWS, HD), 1)
    both = jnp.zeros((ROWS, HD), F32)
    for h, level in zip(heads, levels):
        both = jnp.where(lane % GROUP == h, level, both)
    high = both.astype(BF16).astype(F32)
    middle = (both - high).astype(BF16).astype(F32)
    low = both - high - middle
    picked = jnp.where(lane < GROUP, high, jnp.where(lane < 2 * GROUP, middle, low))
    return jnp.where(lane < 3 * GROUP, picked, 0.0).astype(BF16)


def lse_of(lanes, h):
    return lanes[:, h : h + 1] + lanes[:, GROUP + h : GROUP + h + 1] + lanes[:, 2 * GROUP + h : 2 * GROUP + h + 1]


def image_kernel(shifts, halves, place, lists, counts, *refs):
    number = len(shifts)
    query_refs = refs[: 2 * number]
    own_key, own_value, left, right, far_key, far_value = refs[2 * number : 2 * number + 6]
    key_sources = [(own_key, 0), (left, 0), (far_key, 0), (right, 0)]
    value_sources = [(own_value, 0), (left, HD), (far_value, 0), (right, HD)]
    outs = refs[-11:-9] if halves else refs[-10:-9]
    key_buf, value_buf, row_buf, top_ref, total_ref, work, amount, key_sem, value_sem = refs[-9:]
    z, x = place[0], place[1]
    found = jnp.int32(0)
    for n, shift in enumerate(shifts):
        span = NX * lax.rem(z + shift, NZ) + x
        amount[n] = found
        for back in range(NX):
            image = NX * z + lax.rem(x + NX - back, NX)
            wanted = False
            for j in range(LIST):
                wanted = jnp.logical_or(
                    wanted, jnp.logical_and(j < counts[span], lists[span, j] == image)
                )
            work[found] = back
            found = found + jnp.where(wanted, 1, 0)
    amount[number] = found

    def copies(back, slot):
        return [
            pltpu.make_async_copy(
                source.at[:, :, pl.ds(at, HD)], buffer.at[pl.ds(slot, 1)], sem.at[slot]
            )
            for (source, at), buffer, sem in (
                (key_sources[back], key_buf, key_sem),
                (value_sources[back], value_buf, value_sem),
            )
        ]

    def fetch(entry, slot):
        for back in range(NX):

            @pl.when(entry == back)
            def _(back=back):
                for copy in copies(back, slot):
                    copy.start()

    @pl.when(found > 0)
    def _():
        fetch(work[0], 0)

    for n in range(number):
        for h in range(GROUP):
            side, at = divmod(h, GROUP // 2)
            row_buf[n, h * ROWS : (h + 1) * ROWS, :] = query_refs[2 * n + side][0, :, head_cols(at)]
    top_ref[...] = jnp.full_like(top_ref, START)
    total_ref[...] = jnp.zeros_like(total_ref)

    half = GROUP * ROWS // 2
    for n in range(number):

        def visit(i, carry, n=n):
            slot = lax.rem(i, 2)

            @pl.when(i + 1 < found)
            def _():
                fetch(work[i + 1], 1 - slot)

            for copy in copies(0, slot):
                copy.wait()
            blocks = [row_buf[n, k * half : (k + 1) * half, :] for k in range(2)]
            attend(blocks, key_buf[slot], value_buf[slot], top_ref.at[n], total_ref.at[n])
            return carry

        lax.fori_loop(amount[n], amount[n + 1], visit, 0)

    for n in range(number):
        levels, parts = [], []
        for h in range(GROUP):
            block = slice(h * ROWS, (h + 1) * ROWS)
            row_total = total_ref[n, block, HD:]
            used = row_total > 0.0
            safe = jnp.where(used, row_total, 1.0)
            parts.append((total_ref[n, block, :HD] / safe).astype(BF16))
            levels.append(jnp.where(used, top_ref[n, block, :] + jnp.log2(safe), LOW))
        lanes = lse_lanes(levels, range(GROUP))
        if halves:
            first, second = outs
            for h in range(GROUP // 2):
                first[n, :, head_cols(h)] = parts[h]
                second[n, :, head_cols(h)] = parts[GROUP // 2 + h]
            first[n, :, HALF:] = lanes
            second[n, :, HALF:] = lanes
        else:
            (out,) = outs
            for h in range(GROUP):
                out[n, :, head_cols(h)] = parts[h]
            out[n, :, WIDE:] = lanes


def image_parts(place, lists, counts, images, shifts, queries, earlier, halves=False):
    widths = [HALF_PACK, HALF_PACK] if halves else [PACK]
    number = len(shifts)
    tokens = images[0].shape[1]
    query_specs = [
        pl.BlockSpec((1, ROWS, HALF), lambda i, *_, at=at: (at, 0, 0)) for _, at in queries
    ]
    return pl.pallas_call(
        functools.partial(image_kernel, shifts, halves),
        grid_spec=pltpu.PrefetchScalarGridSpec(
            num_scalar_prefetch=3,
            grid=(1,),
            in_specs=query_specs
            + [pl.BlockSpec(memory_space=pltpu.HBM)] * len(images)
            + [pl.BlockSpec(memory_space=pl.ANY)] * len(earlier),
            out_specs=[pl.BlockSpec((number, ROWS, w), lambda i, *_: (0, 0, 0)) for w in widths],
            scratch_shapes=[
                pltpu.VMEM((2, tokens, HD), BF16),
                pltpu.VMEM((2, tokens, HD), BF16),
                pltpu.VMEM((number, GROUP * ROWS, HD), BF16),
                pltpu.VMEM((number, GROUP * ROWS, HD), F32),
                pltpu.VMEM((number, GROUP * ROWS, 2 * HD), F32),
                pltpu.SMEM((2 * NX + 1,), jnp.int32),
                pltpu.SMEM((number + 1,), jnp.int32),
                pltpu.SemaphoreType.DMA((2,)),
                pltpu.SemaphoreType.DMA((2,)),
            ],
        ),
        out_shape=[jax.ShapeDtypeStruct((number, ROWS, w), BF16) for w in widths],
        compiler_params=pltpu.CompilerParams(vmem_limit_bytes=40 * MIB),
        cost_estimate=pl.CostEstimate(
            flops=number * 10**9, bytes_accessed=number * 2 * 10**6, transcendentals=0
        ),
        name="image_parts_" + "_".join(str(s) for s in shifts),
    )(place, lists, counts, *[a for a, _ in queries], *images, *earlier)


def merged(a, level_a, b, level_b):
    top = jnp.maximum(level_a, level_b)
    share_a, share_b = jnp.exp2(level_a - top), jnp.exp2(level_b - top)
    total = share_a + share_b
    return (share_a * a + share_b * b) / total, top + jnp.log2(total)


def first_merge_kernel(plus_in, minus_in, local_ref, plus_out, minus_out):
    for arrived, side, out, low in (
        (plus_in, 0, plus_out, 0),
        (minus_in, 1, minus_out, GROUP // 2),
    ):
        lanes, own_lanes = arrived[0, :, HALF:].astype(F32), local_ref[side, :, WIDE:].astype(F32)
        levels = []
        for h in range(GROUP):
            own, own_level = local_ref[side, :, head_cols(h)], lse_of(own_lanes, h)
            if low <= h < low + GROUP // 2:
                part, level = merged(
                    arrived[0, :, head_cols(h - low)].astype(F32),
                    lse_of(lanes, h),
                    own.astype(F32),
                    own_level,
                )
                out[0, :, head_cols(h)] = part.astype(BF16)
                levels.append(level)
            else:
                out[0, :, head_cols(h)] = own
                levels.append(own_level)
        out[0, :, WIDE:] = lse_lanes(levels, range(GROUP))


def merge_kernel(plus_in, minus_in, local_ref, plus_out, minus_out):
    for arrived, side, out in ((plus_in, 0, plus_out), (minus_in, 1, minus_out)):
        lanes, own_lanes = arrived[0, :, WIDE:].astype(F32), local_ref[side, :, WIDE:].astype(F32)
        levels = []
        for h in range(GROUP):
            part, level = merged(
                arrived[0, :, head_cols(h)].astype(F32),
                lse_of(lanes, h),
                local_ref[side, :, head_cols(h)].astype(F32),
                lse_of(own_lanes, h),
            )
            out[0, :, head_cols(h)] = part.astype(BF16)
            levels.append(level)
        out[0, :, WIDE:] = lse_lanes(levels, range(GROUP))


def last_merge_kernel(plus_in, minus_in, local_ref, self_ref, out):
    out[:, :WIDE] = self_ref[...]
    lanes = [r[0, :, WIDE:].astype(F32) for r in (plus_in, minus_in, local_ref)]
    for h in range(GROUP):
        part, level = merged(
            plus_in[0, :, head_cols(h)].astype(F32),
            lse_of(lanes[0], h),
            minus_in[0, :, head_cols(h)].astype(F32),
            lse_of(lanes[1], h),
        )
        part, _ = merged(part, level, local_ref[0, :, head_cols(h)].astype(F32), lse_of(lanes[2], h))
        out[:, head_cols(GROUP + h)] = part.astype(BF16)


def small_call(kernel, out_shape, name, *args):
    return pl.pallas_call(
        kernel,
        out_shape=out_shape,
        compiler_params=pltpu.CompilerParams(vmem_limit_bytes=24 * MIB),
        cost_estimate=pl.CostEstimate(flops=10**7, bytes_accessed=2 * 10**6, transcendentals=0),
        name=name,
    )(*args)


def self_kernel(place, starts_ref, query_ref, *refs):
    kv_refs, (out_ref, top_ref, total_ref) = refs[:NX], refs[-3:]
    z, x, earliest = place[0], place[1], place[2]
    first = (NX * z + x) * ROWS
    top_ref[...] = jnp.full_like(top_ref, START)
    total_ref[...] = jnp.zeros_like(total_ref)
    chunks = (z - earliest // (NX * ROWS)) // 2 + 1
    half = GROUP // 2
    blocks = [
        jnp.concatenate([query_ref[:, head_cols(half * n + k)] for k in range(half)], axis=0)
        for n in range(2)
    ]
    for size in range(1, KV_ROWS // 2 + 1):

        @pl.when(chunks == size)
        def _(size=size):
            rows = 2 * size
            column_keys = rows * ROWS
            shape = (ROWS, NX * column_keys)
            step = lax.broadcasted_iota(jnp.int32, shape, 1)
            back = sum((step >= k * column_keys).astype(jnp.int32) for k in range(1, NX))
            inner = step - back * column_keys
            up = inner // ROWS
            column = x - back
            column = jnp.where(column < 0, column + NX, column)
            key_pos = (NX * (z - up) + column) * ROWS + inner - up * ROWS
            row_pos = first + lax.broadcasted_iota(jnp.int32, shape, 0)
            seen = jnp.logical_and(key_pos <= row_pos, key_pos >= starts_ref[:, :1])
            bias = jnp.where(seen, 0.0, LOW)
            bias = jnp.concatenate([bias] * half, axis=0)
            loaded = [ref[r] for ref in kv_refs for r in range(rows)]
            keys = jnp.concatenate([block[:, :HD] for block in loaded], axis=0)
            values = jnp.concatenate([block[:, HD:] for block in loaded], axis=0)
            attend(blocks, keys, values, top_ref, total_ref, bias)

    for h in range(GROUP):
        block = pl.ds(h * ROWS, ROWS)
        out_ref[:, head_cols(h)] = (total_ref[block, :HD] / total_ref[block, HD:]).astype(BF16)


def self_attention(place, starts, queries, kv, earlier):
    vmem = pl.BlockSpec(memory_space=pltpu.VMEM)
    return pl.pallas_call(
        self_kernel,
        grid_spec=pltpu.PrefetchScalarGridSpec(
            num_scalar_prefetch=1,
            grid=(),
            in_specs=[vmem] * (2 + NX) + [pl.BlockSpec(memory_space=pl.ANY)],
            out_specs=vmem,
            scratch_shapes=[
                pltpu.VMEM((GROUP * ROWS, HD), F32),
                pltpu.VMEM((GROUP * ROWS, 2 * HD), F32),
            ],
        ),
        out_shape=jax.ShapeDtypeStruct((ROWS, WIDE), BF16),
        compiler_params=pltpu.CompilerParams(vmem_limit_bytes=48 * MIB),
        cost_estimate=pl.CostEstimate(
            flops=2 * 10**9, bytes_accessed=4 * 10**6, transcendentals=0
        ),
        name="self_attention",
    )(place, starts, queries, *kv, earlier)


def on_device(
    self_queries,
    self_keys,
    self_values,
    cross_queries,
    image_keys,
    image_values,
    image_lists,
    image_counts,
    doc_ids,
):
    span = lax.axis_index("ctx")
    own_docs = lax.dynamic_slice_in_dim(doc_ids, span * ROWS, ROWS)
    starts = jnp.sum((doc_ids[None, :] < own_docs[:, None]).astype(jnp.int32), axis=1)
    place = jnp.stack([span // NX, span % NX, starts[0]]).astype(jnp.int32)
    starts = jnp.broadcast_to(starts[:, None], (ROWS, HD))

    sent = jnp.stack(
        [
            jnp.concatenate([cross_queries[:, :HALF], self_keys], axis=1),
            jnp.concatenate([cross_queries[:, HALF:], self_values], axis=1),
        ]
    )
    own_image = jnp.concatenate([image_keys, image_values], axis=2)
    left, right = moved(own_image, 0, 1), moved(own_image, 0, -1)
    images = [
        image_keys,
        image_values,
        left,
        right,
        moved(left[:, :, :HD], 0, 1),
        moved(right[:, :, HD:], 0, -1),
    ]
    before, after = [sent], [sent]
    for _ in range(3):
        before.append(moved(before[-1], 1, 0))
        after.append(moved(after[-1], -1, 0))
    far_first = moved(before[3][:1], 1, 0)
    far_second = moved(after[3][1:], -1, 0)

    kv_rows = [(block[0], block[1]) for block in before] + [
        (far_first[0], far_second[0]),
        (after[3][0], after[3][1]),
    ]
    own_kv = jnp.stack([jnp.concatenate([a[:, HALF:], b[:, HALF:]], axis=1) for a, b in kv_rows])
    kv = [own_kv] + [moved(own_kv, 0, k) for k in (1, 2, 3)]

    parts = functools.partial(image_parts, place, image_lists, image_counts, images)
    full = jax.ShapeDtypeStruct((1, ROWS, PACK), BF16)
    plus, minus = parts((4,), [(far_first, 0), (far_second, 0)], [], halves=True)
    last = plus
    plus, minus = moved(plus, 1, 0), moved(minus, -1, 0)
    for distance in (3, 2, 1):
        (local,) = parts(
            (distance, NZ - distance),
            [(block[distance], side) for block in (after, before) for side in (0, 1)],
            [last],
        )
        kernel = first_merge_kernel if distance == 3 else merge_kernel
        last, other = small_call(
            kernel, (full, full), f"merge_{distance}", plus, minus, local
        )
        plus, minus = moved(last, 1, 0), moved(other, -1, 0)
    (local,) = parts((0,), [(sent, 0), (sent, 1)], [last])
    self_out = self_attention(place, starts, self_queries, kv, local)
    both = small_call(
        last_merge_kernel,
        jax.ShapeDtypeStruct((ROWS, 2 * WIDE), BF16),
        "merge_0",
        plus,
        minus,
        local,
        self_out,
    )
    back = lax.all_to_all(
        both.reshape(GROUP, ROWS // GROUP, 2 * WIDE), "head", split_axis=0, concat_axis=0
    )
    return tuple(
        jnp.swapaxes(back[:, :, k * WIDE : (k + 1) * WIDE], 0, 1).reshape(
            ROWS // GROUP, GROUP * WIDE
        )
        for k in range(2)
    )


def solution(mesh):
    in_specs = (
        P("ctx", "head"),
        P("ctx", "head"),
        P("ctx", "head"),
        P("ctx", "head"),
        P("ctx", None, "head"),
        P("ctx", None, "head"),
        P(),
        P(),
        P(),
    )
    out_specs = (P(("ctx", "head"), None), P(("ctx", "head"), None))
    return jax.shard_map(
        on_device, mesh=mesh, in_specs=in_specs, out_specs=out_specs, check_vma=False
    )
```

```python
import functools
import math

import jax
import jax.numpy as jnp
from jax import lax
from jax.experimental import pallas as pl
from jax.experimental.pallas import tpu as pltpu
from jax.sharding import PartitionSpec as P

HD = 128
LIST = 6
GROUP = 8
ROWS = 128
NX = 4
NZ = 8
WIDE = GROUP * HD
HALF = WIDE // 2
PACK = WIDE + HD
HALF_PACK = HALF + HD
KV_ROWS = 6
LOW = -1e30
START = -1e29
SCALE2 = math.log2(math.e) / math.sqrt(HD)
MIB = 1024 * 1024
F32 = jnp.float32
BF16 = jnp.bfloat16

def moved(array, dz, dx):
    pairs = [
        (NX * z + x, NX * ((z + dz) % NZ) + (x + dx) % NX) for z in range(NZ) for x in range(NX)
    ]
    return lax.ppermute(array, "ctx", pairs)


def nt(a, b):
    return lax.dot_general(a, b, (((1,), (1,)), ((), ())), preferred_element_type=F32)


def nn(a, b):
    return lax.dot_general(a, b, (((1,), (0,)), ((), ())), preferred_element_type=F32)


def attend(query_blocks, keys, values, top_ref, total_ref, bias=None):
    wide_values = jnp.concatenate([values, jnp.ones_like(values)], axis=1)
    rows = query_blocks[0].shape[0]
    ahead = nt(query_blocks[0], keys)
    for n in range(len(query_blocks)):
        scores = ahead
        if n + 1 < len(query_blocks):
            ahead = nt(query_blocks[n + 1], keys)
        block = slice(n * rows, (n + 1) * rows)
        if bias is not None:
            scores = scores + bias
        old = top_ref[block, :]
        new = jnp.maximum(old, jnp.max(scores, axis=1, keepdims=True) * SCALE2)
        weights = jnp.exp2(scores * SCALE2 - new[:, :1]).astype(BF16)
        fade = jnp.exp2(old - new)
        total_ref[block, :] = total_ref[block, :] * jnp.concatenate([fade, fade], axis=1) + nn(
            weights, wide_values
        )
        top_ref[block, :] = new


def head_cols(h):
    return slice(h * HD, (h + 1) * HD)


def lane_index():
    return lax.broadcasted_iota(jnp.int32, (ROWS, HD), 1)


def level_terms(levels):
    levels = jnp.where(lane_index() < GROUP, levels, 0.0)
    high = levels.astype(BF16).astype(F32)
    middle = (levels - high).astype(BF16).astype(F32)
    low = levels - high - middle
    terms = high + pltpu.roll(middle, GROUP, 1) + pltpu.roll(low, 2 * GROUP, 1)
    return terms.astype(BF16)


def levels_of(terms):
    terms = terms.astype(F32)
    return terms + pltpu.roll(terms, HD - GROUP, 1) + pltpu.roll(terms, HD - 2 * GROUP, 1)


def image_kernel(shifts, halves, backs, started, place, lists, counts, *refs):
    number = len(shifts)
    query_refs = refs[: 2 * number]
    sources = dict(zip(image_names(backs), refs[2 * number :]))
    key_sources = [("own_key", 0), ("left", 0), ("far_key", 0), ("right", 0)]
    value_sources = [("own_value", 0), ("left", HD), ("far_value", 0), ("right", HD)]
    start_ref = refs[2 * number + len(sources)] if started else None
    outs = refs[-11:-9] if halves else refs[-10:-9]
    key_buf, value_buf, row_buf, top_ref, total_ref, work, amount, key_sem, value_sem = refs[-9:]
    z, x = place[0], place[1]
    found = jnp.int32(0)
    for n, shift in enumerate(shifts):
        span = NX * lax.rem(z + shift, NZ) + x
        amount[n] = found
        for back in backs:
            image = NX * z + lax.rem(x + NX - back, NX)
            wanted = False
            for j in range(LIST):
                wanted = jnp.logical_or(
                    wanted, jnp.logical_and(j < counts[span], lists[span, j] == image)
                )
            work[found] = back
            found = found + jnp.where(wanted, 1, 0)
    amount[number] = found

    def copies(back, slot):
        return [
            pltpu.make_async_copy(
                sources[name].at[:, :, pl.ds(at, HD)], buffer.at[pl.ds(slot, 1)], sem.at[slot]
            )
            for (name, at), buffer, sem in (
                (key_sources[back], key_buf, key_sem),
                (value_sources[back], value_buf, value_sem),
            )
        ]

    def fetch(entry, slot):
        for back in backs:

            @pl.when(entry == back)
            def _(back=back):
                for copy in copies(back, slot):
                    copy.start()

    @pl.when(found > 0)
    def _():
        fetch(work[0], 0)

    for n in range(number):
        for h in range(GROUP):
            side, at = divmod(h, GROUP // 2)
            row_buf[n, h * ROWS : (h + 1) * ROWS, :] = query_refs[2 * n + side][0, :, head_cols(at)]
    if started:
        for n in range(number):
            levels = levels_of(start_ref[n, :, WIDE:])
            for h in range(GROUP):
                block = slice(h * ROWS, (h + 1) * ROWS)
                level = jnp.broadcast_to(levels[:, h : h + 1], (ROWS, HD))
                used = level > START
                top_ref[n, block, :] = jnp.where(used, level, START)
                total_ref[n, block, :HD] = start_ref[n, :, head_cols(h)].astype(F32)
                total_ref[n, block, HD:] = jnp.where(used, 1.0, 0.0)
    else:
        top_ref[...] = jnp.full_like(top_ref, START)
        total_ref[...] = jnp.zeros_like(total_ref)

    half = GROUP * ROWS // 2
    for n in range(number):

        def visit(i, carry, n=n):
            slot = lax.rem(i, 2)

            @pl.when(i + 1 < found)
            def _():
                fetch(work[i + 1], 1 - slot)

            for copy in copies(backs[0], slot):
                copy.wait()
            blocks = [row_buf[n, k * half : (k + 1) * half, :] for k in range(2)]
            attend(blocks, key_buf[slot], value_buf[slot], top_ref.at[n], total_ref.at[n])
            return carry

        lax.fori_loop(amount[n], amount[n + 1], visit, 0)

    for n in range(number):
        lane = lane_index()
        parts, top_lanes, total_lanes = [], jnp.zeros((ROWS, HD), F32), jnp.zeros((ROWS, HD), F32)
        for h in range(GROUP):
            block = slice(h * ROWS, (h + 1) * ROWS)
            row_total = total_ref[n, block, HD:]
            top_lanes = jnp.where(lane == h, top_ref[n, block, :], top_lanes)
            total_lanes = jnp.where(lane == h, row_total, total_lanes)
            safe = jnp.where(row_total > 0.0, row_total, 1.0)
            parts.append((total_ref[n, block, :HD] / safe).astype(BF16))
        used = total_lanes > 0.0
        lanes = level_terms(
            jnp.where(used, top_lanes + jnp.log2(jnp.where(used, total_lanes, 1.0)), LOW)
        )
        if halves:
            first, second = outs
            for h in range(GROUP // 2):
                first[n, :, head_cols(h)] = parts[h]
                second[n, :, head_cols(h)] = parts[GROUP // 2 + h]
            first[n, :, HALF:] = lanes
            second[n, :, HALF:] = lanes
        else:
            (out,) = outs
            for h in range(GROUP):
                out[n, :, head_cols(h)] = parts[h]
            out[n, :, WIDE:] = lanes


def image_names(backs):
    names = ["own_key", "own_value"] if 0 in backs else []
    names += ["left"] if 1 in backs else []
    names += ["right"] if 3 in backs else []
    return names + (["far_key", "far_value"] if 2 in backs else [])


def image_parts(
    place, lists, counts, images, shifts, queries, earlier, halves=False, backs=(0, 1, 2, 3), start=None
):
    widths = [HALF_PACK, HALF_PACK] if halves else [PACK]
    number = len(shifts)
    tokens = images["own_key"].shape[1]
    chosen = [images[name] for name in image_names(backs)]
    starts = [] if start is None else [start]
    query_specs = [
        pl.BlockSpec((1, ROWS, HALF), lambda i, *_, at=at: (at, 0, 0)) for _, at in queries
    ]
    return pl.pallas_call(
        functools.partial(image_kernel, shifts, halves, backs, start is not None),
        grid_spec=pltpu.PrefetchScalarGridSpec(
            num_scalar_prefetch=3,
            grid=(1,),
            in_specs=query_specs
            + [pl.BlockSpec(memory_space=pltpu.HBM)] * len(chosen)
            + [pl.BlockSpec((number, ROWS, PACK), lambda i, *_: (0, 0, 0))] * len(starts)
            + [pl.BlockSpec(memory_space=pl.ANY)] * len(earlier),
            out_specs=[pl.BlockSpec((number, ROWS, w), lambda i, *_: (0, 0, 0)) for w in widths],
            scratch_shapes=[
                pltpu.VMEM((2, tokens, HD), BF16),
                pltpu.VMEM((2, tokens, HD), BF16),
                pltpu.VMEM((number, GROUP * ROWS, HD), BF16),
                pltpu.VMEM((number, GROUP * ROWS, HD), F32),
                pltpu.VMEM((number, GROUP * ROWS, 2 * HD), F32),
                pltpu.SMEM((2 * NX + 1,), jnp.int32),
                pltpu.SMEM((number + 1,), jnp.int32),
                pltpu.SemaphoreType.DMA((2,)),
                pltpu.SemaphoreType.DMA((2,)),
            ],
        ),
        out_shape=[jax.ShapeDtypeStruct((number, ROWS, w), BF16) for w in widths],
        compiler_params=pltpu.CompilerParams(vmem_limit_bytes=40 * MIB),
        cost_estimate=pl.CostEstimate(
            flops=number * 10**9, bytes_accessed=number * 2 * 10**6, transcendentals=0
        ),
        name="image_parts_" + "_".join(str(s) for s in shifts) + ("" if 2 in backs else "_near"),
    )(place, lists, counts, *[a for a, _ in queries], *chosen, *starts, *earlier)


def shares_of(*levels):
    top = functools.reduce(jnp.maximum, levels)
    grown = [jnp.exp2(level - top) for level in levels]
    total = sum(grown)
    return [g / total for g in grown], top + jnp.log2(total)


def first_merge_kernel(plus_in, minus_in, local_ref, plus_out, minus_out):
    lane = lane_index()
    for arrived, side, out, low in (
        (plus_in, 0, plus_out, 0),
        (minus_in, 1, minus_out, GROUP // 2),
    ):
        sent = jnp.logical_and(lane >= low, lane < low + GROUP // 2)
        (share, own_share), levels = shares_of(
            jnp.where(sent, levels_of(arrived[0, :, HALF:]), LOW),
            levels_of(local_ref[side, :, WIDE:]),
        )
        for h in range(GROUP):
            own = local_ref[side, :, head_cols(h)]
            if low <= h < low + GROUP // 2:
                part = share[:, h : h + 1] * arrived[0, :, head_cols(h - low)].astype(F32)
                own = (part + own_share[:, h : h + 1] * own.astype(F32)).astype(BF16)
            out[0, :, head_cols(h)] = own
        out[0, :, WIDE:] = level_terms(levels)


def merge_kernel(plus_in, minus_in, local_ref, plus_out, minus_out):
    for arrived, side, out in ((plus_in, 0, plus_out), (minus_in, 1, minus_out)):
        (share, own_share), levels = shares_of(
            levels_of(arrived[0, :, WIDE:]), levels_of(local_ref[side, :, WIDE:])
        )
        for h in range(GROUP):
            part = share[:, h : h + 1] * arrived[0, :, head_cols(h)].astype(F32)
            own = own_share[:, h : h + 1] * local_ref[side, :, head_cols(h)].astype(F32)
            out[0, :, head_cols(h)] = (part + own).astype(BF16)
        out[0, :, WIDE:] = level_terms(levels)


def last_merge_kernel(plus_in, minus_in, local_ref, self_ref, out):
    out[:, :WIDE] = self_ref[...]
    packs = (plus_in, minus_in, local_ref)
    shares, _ = shares_of(*[levels_of(r[0, :, WIDE:]) for r in packs])
    for h in range(GROUP):
        part = sum(
            share[:, h : h + 1] * r[0, :, head_cols(h)].astype(F32)
            for share, r in zip(shares, packs)
        )
        out[:, head_cols(GROUP + h)] = part.astype(BF16)


def small_call(kernel, out_shape, name, *args):
    return pl.pallas_call(
        kernel,
        out_shape=out_shape,
        compiler_params=pltpu.CompilerParams(vmem_limit_bytes=24 * MIB),
        cost_estimate=pl.CostEstimate(flops=10**7, bytes_accessed=2 * 10**6, transcendentals=0),
        name=name,
    )(*args)


def self_kernel(place, starts_ref, query_ref, *refs):
    kv_refs, (out_ref, top_ref, total_ref) = refs[:NX], refs[-3:]
    z, x, earliest = place[0], place[1], place[2]
    first = (NX * z + x) * ROWS
    top_ref[...] = jnp.full_like(top_ref, START)
    total_ref[...] = jnp.zeros_like(total_ref)
    chunks = (z - earliest // (NX * ROWS)) // 2 + 1
    half = GROUP // 2
    blocks = [
        jnp.concatenate([query_ref[:, head_cols(half * n + k)] for k in range(half)], axis=0)
        for n in range(2)
    ]
    for size in range(1, KV_ROWS // 2 + 1):

        @pl.when(chunks == size)
        def _(size=size):
            rows = 2 * size
            column_keys = rows * ROWS
            shape = (ROWS, NX * column_keys)
            step = lax.broadcasted_iota(jnp.int32, shape, 1)
            back = sum((step >= k * column_keys).astype(jnp.int32) for k in range(1, NX))
            inner = step - back * column_keys
            up = inner // ROWS
            column = x - back
            column = jnp.where(column < 0, column + NX, column)
            key_pos = (NX * (z - up) + column) * ROWS + inner - up * ROWS
            row_pos = first + lax.broadcasted_iota(jnp.int32, shape, 0)
            seen = jnp.logical_and(key_pos <= row_pos, key_pos >= starts_ref[:, :1])
            bias = jnp.where(seen, 0.0, LOW)
            bias = jnp.concatenate([bias] * half, axis=0)
            loaded = [ref[r] for ref in kv_refs for r in range(rows)]
            keys = jnp.concatenate([block[:, :HD] for block in loaded], axis=0)
            values = jnp.concatenate([block[:, HD:] for block in loaded], axis=0)
            attend(blocks, keys, values, top_ref, total_ref, bias)

    for h in range(GROUP):
        block = pl.ds(h * ROWS, ROWS)
        out_ref[:, head_cols(h)] = (total_ref[block, :HD] / total_ref[block, HD:]).astype(BF16)


def self_attention(place, starts, queries, kv, earlier):
    vmem = pl.BlockSpec(memory_space=pltpu.VMEM)
    return pl.pallas_call(
        self_kernel,
        grid_spec=pltpu.PrefetchScalarGridSpec(
            num_scalar_prefetch=1,
            grid=(),
            in_specs=[vmem] * (2 + NX) + [pl.BlockSpec(memory_space=pl.ANY)],
            out_specs=vmem,
            scratch_shapes=[
                pltpu.VMEM((GROUP * ROWS, HD), F32),
                pltpu.VMEM((GROUP * ROWS, 2 * HD), F32),
            ],
        ),
        out_shape=jax.ShapeDtypeStruct((ROWS, WIDE), BF16),
        compiler_params=pltpu.CompilerParams(vmem_limit_bytes=48 * MIB),
        cost_estimate=pl.CostEstimate(
            flops=2 * 10**9, bytes_accessed=4 * 10**6, transcendentals=0
        ),
        name="self_attention",
    )(place, starts, queries, *kv, earlier)


def on_device(
    self_queries,
    self_keys,
    self_values,
    cross_queries,
    image_keys,
    image_values,
    image_lists,
    image_counts,
    doc_ids,
):
    span = lax.axis_index("ctx")
    own_docs = lax.dynamic_slice_in_dim(doc_ids, span * ROWS, ROWS)
    starts = jnp.sum((doc_ids[None, :] < own_docs[:, None]).astype(jnp.int32), axis=1)
    place = jnp.stack([span // NX, span % NX, starts[0]]).astype(jnp.int32)
    starts = jnp.broadcast_to(starts[:, None], (ROWS, HD))

    sent = jnp.stack(
        [
            jnp.concatenate([cross_queries[:, :HALF], self_keys], axis=1),
            jnp.concatenate([cross_queries[:, HALF:], self_values], axis=1),
        ]
    )
    own_image = jnp.concatenate([image_keys, image_values], axis=2)
    left, right = moved(own_image, 0, 1), moved(own_image, 0, -1)
    images = {
        "own_key": image_keys,
        "own_value": image_values,
        "left": left,
        "right": right,
        "far_key": moved(left[:, :, :HD], 0, 1),
        "far_value": moved(right[:, :, HD:], 0, -1),
    }
    before, after = [sent], [sent]
    for _ in range(3):
        before.append(moved(before[-1], 1, 0))
        after.append(moved(after[-1], -1, 0))
    far_first = moved(before[3][:1], 1, 0)
    far_second = moved(after[3][1:], -1, 0)

    kv_rows = [(block[0], block[1]) for block in before] + [
        (far_first[0], far_second[0]),
        (after[3][0], after[3][1]),
    ]
    own_kv = jnp.stack([jnp.concatenate([a[:, HALF:], b[:, HALF:]], axis=1) for a, b in kv_rows])
    kv = [own_kv] + [moved(own_kv, 0, k) for k in (1, 2, 3)]

    parts = functools.partial(image_parts, place, image_lists, image_counts, images)
    full = jax.ShapeDtypeStruct((1, ROWS, PACK), BF16)

    def queries_at(distance):
        return [(block[distance], side) for block in (after, before) for side in (0, 1)]

    (near,) = parts((3, NZ - 3), queries_at(3), [], backs=(0, 1, 3))
    plus, minus = parts((4,), [(far_first, 0), (far_second, 0)], [near], halves=True)
    last = plus
    plus, minus = moved(plus, 1, 0), moved(minus, -1, 0)
    for distance in (3, 2, 1):
        chosen = {"backs": (2,), "start": near} if distance == 3 else {}
        (local,) = parts((distance, NZ - distance), queries_at(distance), [last], **chosen)
        kernel = first_merge_kernel if distance == 3 else merge_kernel
        last, other = small_call(kernel, (full, full), f"merge_{distance}", plus, minus, local)
        plus, minus = moved(last, 1, 0), moved(other, -1, 0)
    (local,) = parts((0,), [(sent, 0), (sent, 1)], [last])
    self_out = self_attention(place, starts, self_queries, kv, local)
    both = small_call(
        last_merge_kernel,
        jax.ShapeDtypeStruct((ROWS, 2 * WIDE), BF16),
        "merge_0",
        plus,
        minus,
        local,
        self_out,
    )
    back = lax.all_to_all(
        both.reshape(GROUP, ROWS // GROUP, 2 * WIDE), "head", split_axis=0, concat_axis=0
    )
    return tuple(
        jnp.swapaxes(back[:, :, k * WIDE : (k + 1) * WIDE], 0, 1).reshape(
            ROWS // GROUP, GROUP * WIDE
        )
        for k in range(2)
    )


def solution(mesh):
    in_specs = (
        P("ctx", "head"),
        P("ctx", "head"),
        P("ctx", "head"),
        P("ctx", "head"),
        P("ctx", None, "head"),
        P("ctx", None, "head"),
        P(),
        P(),
        P(),
    )
    out_specs = (P(("ctx", "head"), None), P(("ctx", "head"), None))
    return jax.shard_map(
        on_device, mesh=mesh, in_specs=in_specs, out_specs=out_specs, check_vma=False
    )
```

```python
import functools
import math

import jax
import jax.numpy as jnp
from jax import lax
from jax.experimental import pallas as pl
from jax.experimental.pallas import tpu as pltpu
from jax.sharding import PartitionSpec as P

HD = 128
LIST = 6
GROUP = 8
ROWS = 128
NX = 4
NZ = 8
WIDE = GROUP * HD
HALF = WIDE // 2
PACK = WIDE + HD
HALF_PACK = HALF + HD
KV_ROWS = 6
LOW = -1e30
START = -1e29
SCALE2 = math.log2(math.e) / math.sqrt(HD)
MIB = 1024 * 1024
F32 = jnp.float32
BF16 = jnp.bfloat16

def moved(array, dz, dx):
    pairs = [
        (NX * z + x, NX * ((z + dz) % NZ) + (x + dx) % NX) for z in range(NZ) for x in range(NX)
    ]
    return lax.ppermute(array, "ctx", pairs)


def nt(a, b):
    return lax.dot_general(a, b, (((1,), (1,)), ((), ())), preferred_element_type=F32)


def nn(a, b):
    return lax.dot_general(a, b, (((1,), (0,)), ((), ())), preferred_element_type=F32)


def attend(query_blocks, keys, values, top_ref, total_ref, bias=None):
    wide_values = jnp.concatenate([values, jnp.ones_like(values)], axis=1)
    rows = query_blocks[0].shape[0]
    ahead = nt(query_blocks[0], keys)
    for n in range(len(query_blocks)):
        scores = ahead
        if n + 1 < len(query_blocks):
            ahead = nt(query_blocks[n + 1], keys)
        block = slice(n * rows, (n + 1) * rows)
        if bias is not None:
            scores = scores + bias
        old = top_ref[block, :]
        new = jnp.maximum(old, jnp.max(scores, axis=1, keepdims=True) * SCALE2)
        weights = jnp.exp2(scores * SCALE2 - new[:, :1]).astype(BF16)
        fade = jnp.exp2(old - new)
        total_ref[block, :] = total_ref[block, :] * jnp.concatenate([fade, fade], axis=1) + nn(
            weights, wide_values
        )
        top_ref[block, :] = new


def head_cols(h):
    return slice(h * HD, (h + 1) * HD)


def lane_index():
    return lax.broadcasted_iota(jnp.int32, (ROWS, HD), 1)


def level_terms(levels):
    levels = jnp.where(lane_index() < GROUP, levels, 0.0)
    high = levels.astype(BF16).astype(F32)
    middle = (levels - high).astype(BF16).astype(F32)
    low = levels - high - middle
    terms = high + pltpu.roll(middle, GROUP, 1) + pltpu.roll(low, 2 * GROUP, 1)
    return terms.astype(BF16)


def levels_of(terms):
    terms = terms.astype(F32)
    return terms + pltpu.roll(terms, HD - GROUP, 1) + pltpu.roll(terms, HD - 2 * GROUP, 1)


def image_kernel(shifts, halves, backs, started, place, lists, counts, *refs):
    number = len(shifts)
    query_refs = refs[: 2 * number]
    sources = dict(zip(image_names(backs), refs[2 * number :]))
    key_sources = [("own_key", 0), ("left", 0), ("far_key", 0), ("right", 0)]
    value_sources = [("own_value", 0), ("left", HD), ("far_value", 0), ("right", HD)]
    start_ref = refs[2 * number + len(sources)] if started else None
    outs = refs[-11:-9] if halves else refs[-10:-9]
    key_buf, value_buf, row_buf, top_ref, total_ref, work, amount, key_sem, value_sem = refs[-9:]
    z, x = place[0], place[1]
    found = jnp.int32(0)
    for n, shift in enumerate(shifts):
        span = NX * lax.rem(z + shift, NZ) + x
        amount[n] = found
        for back in backs:
            image = NX * z + lax.rem(x + NX - back, NX)
            wanted = False
            for j in range(LIST):
                wanted = jnp.logical_or(
                    wanted, jnp.logical_and(j < counts[span], lists[span, j] == image)
                )
            work[found] = back
            found = found + jnp.where(wanted, 1, 0)
    amount[number] = found

    def copies(back, slot):
        return [
            pltpu.make_async_copy(
                sources[name].at[:, :, pl.ds(at, HD)], buffer.at[pl.ds(slot, 1)], sem.at[slot]
            )
            for (name, at), buffer, sem in (
                (key_sources[back], key_buf, key_sem),
                (value_sources[back], value_buf, value_sem),
            )
        ]

    def fetch(entry, slot):
        for back in backs:

            @pl.when(entry == back)
            def _(back=back):
                for copy in copies(back, slot):
                    copy.start()

    @pl.when(found > 0)
    def _():
        fetch(work[0], 0)

    for n in range(number):
        for h in range(GROUP):
            side, at = divmod(h, GROUP // 2)
            row_buf[n, h * ROWS : (h + 1) * ROWS, :] = query_refs[2 * n + side][0, :, head_cols(at)]
    if started:
        for n in range(number):
            levels = levels_of(start_ref[n, :, WIDE:])
            for h in range(GROUP):
                block = slice(h * ROWS, (h + 1) * ROWS)
                level = jnp.broadcast_to(levels[:, h : h + 1], (ROWS, HD))
                used = level > START
                top_ref[n, block, :] = jnp.where(used, level, START)
                total_ref[n, block, :HD] = start_ref[n, :, head_cols(h)].astype(F32)
                total_ref[n, block, HD:] = jnp.where(used, 1.0, 0.0)
    else:
        top_ref[...] = jnp.full_like(top_ref, START)
        total_ref[...] = jnp.zeros_like(total_ref)

    half = GROUP * ROWS // 2
    for n in range(number):

        def visit(i, carry, n=n):
            slot = lax.rem(i, 2)

            @pl.when(i + 1 < found)
            def _():
                fetch(work[i + 1], 1 - slot)

            for copy in copies(backs[0], slot):
                copy.wait()
            blocks = [row_buf[n, k * half : (k + 1) * half, :] for k in range(2)]
            attend(blocks, key_buf[slot], value_buf[slot], top_ref.at[n], total_ref.at[n])
            return carry

        lax.fori_loop(amount[n], amount[n + 1], visit, 0)

    for n in range(number):
        lane = lane_index()
        parts, top_lanes, total_lanes = [], jnp.zeros((ROWS, HD), F32), jnp.zeros((ROWS, HD), F32)
        for h in range(GROUP):
            block = slice(h * ROWS, (h + 1) * ROWS)
            row_total = total_ref[n, block, HD:]
            top_lanes = jnp.where(lane == h, top_ref[n, block, :], top_lanes)
            total_lanes = jnp.where(lane == h, row_total, total_lanes)
            safe = jnp.where(row_total > 0.0, row_total, 1.0)
            parts.append((total_ref[n, block, :HD] / safe).astype(BF16))
        used = total_lanes > 0.0
        lanes = level_terms(
            jnp.where(used, top_lanes + jnp.log2(jnp.where(used, total_lanes, 1.0)), LOW)
        )
        if halves:
            first, second = outs
            for h in range(GROUP // 2):
                first[n, :, head_cols(h)] = parts[h]
                second[n, :, head_cols(h)] = parts[GROUP // 2 + h]
            first[n, :, HALF:] = lanes
            second[n, :, HALF:] = lanes
        else:
            (out,) = outs
            for h in range(GROUP):
                out[n, :, head_cols(h)] = parts[h]
            out[n, :, WIDE:] = lanes


def image_names(backs):
    names = ["own_key", "own_value"] if 0 in backs else []
    names += ["left"] if 1 in backs else []
    names += ["right"] if 3 in backs else []
    return names + (["far_key", "far_value"] if 2 in backs else [])


def image_parts(
    place, lists, counts, images, shifts, queries, earlier, halves=False, backs=(0, 1, 2, 3), start=None
):
    widths = [HALF_PACK, HALF_PACK] if halves else [PACK]
    number = len(shifts)
    tokens = images["own_key"].shape[1]
    chosen = [images[name] for name in image_names(backs)]
    starts = [] if start is None else [start]
    query_specs = [
        pl.BlockSpec((1, ROWS, HALF), lambda i, *_, at=at: (at, 0, 0)) for _, at in queries
    ]
    return pl.pallas_call(
        functools.partial(image_kernel, shifts, halves, backs, start is not None),
        grid_spec=pltpu.PrefetchScalarGridSpec(
            num_scalar_prefetch=3,
            grid=(1,),
            in_specs=query_specs
            + [pl.BlockSpec(memory_space=pltpu.HBM)] * len(chosen)
            + [pl.BlockSpec((number, ROWS, PACK), lambda i, *_: (0, 0, 0))] * len(starts)
            + [pl.BlockSpec(memory_space=pl.ANY)] * len(earlier),
            out_specs=[pl.BlockSpec((number, ROWS, w), lambda i, *_: (0, 0, 0)) for w in widths],
            scratch_shapes=[
                pltpu.VMEM((2, tokens, HD), BF16),
                pltpu.VMEM((2, tokens, HD), BF16),
                pltpu.VMEM((number, GROUP * ROWS, HD), BF16),
                pltpu.VMEM((number, GROUP * ROWS, HD), F32),
                pltpu.VMEM((number, GROUP * ROWS, 2 * HD), F32),
                pltpu.SMEM((number * NX + 1,), jnp.int32),
                pltpu.SMEM((number + 1,), jnp.int32),
                pltpu.SemaphoreType.DMA((2,)),
                pltpu.SemaphoreType.DMA((2,)),
            ],
        ),
        out_shape=[jax.ShapeDtypeStruct((number, ROWS, w), BF16) for w in widths],
        compiler_params=pltpu.CompilerParams(vmem_limit_bytes=40 * MIB),
        cost_estimate=pl.CostEstimate(
            flops=number * 10**9, bytes_accessed=number * 2 * 10**6, transcendentals=0
        ),
        name="image_parts_" + "_".join(str(s) for s in shifts) + ("" if 2 in backs else "_near"),
    )(place, lists, counts, *[a for a, _ in queries], *chosen, *starts, *earlier)


def shares_of(*levels):
    top = functools.reduce(jnp.maximum, levels)
    grown = [jnp.exp2(level - top) for level in levels]
    total = sum(grown)
    return [g / total for g in grown], top + jnp.log2(total)


def first_merge_kernel(side, arrived, local_ref, out):
    lane = lane_index()
    low = side * GROUP // 2
    sent = jnp.logical_and(lane >= low, lane < low + GROUP // 2)
    (share, own_share), levels = shares_of(
        jnp.where(sent, levels_of(arrived[0, :, HALF:]), LOW),
        levels_of(local_ref[side, :, WIDE:]),
    )
    for h in range(GROUP):
        own = local_ref[side, :, head_cols(h)]
        if low <= h < low + GROUP // 2:
            part = share[:, h : h + 1] * arrived[0, :, head_cols(h - low)].astype(F32)
            own = (part + own_share[:, h : h + 1] * own.astype(F32)).astype(BF16)
        out[0, :, head_cols(h)] = own
    out[0, :, WIDE:] = level_terms(levels)


def merge_kernel(side, arrived, local_ref, out):
    (share, own_share), levels = shares_of(
        levels_of(arrived[0, :, WIDE:]), levels_of(local_ref[side, :, WIDE:])
    )
    for h in range(GROUP):
        part = share[:, h : h + 1] * arrived[0, :, head_cols(h)].astype(F32)
        own = own_share[:, h : h + 1] * local_ref[side, :, head_cols(h)].astype(F32)
        out[0, :, head_cols(h)] = (part + own).astype(BF16)
    out[0, :, WIDE:] = level_terms(levels)


def last_merge_kernel(plus_in, minus_in, local_ref, self_ref, out):
    out[:, :WIDE] = self_ref[...]
    packs = (plus_in, minus_in, local_ref)
    shares, _ = shares_of(*[levels_of(r[r.shape[0] - 1, :, WIDE:]) for r in packs])
    for h in range(GROUP):
        part = sum(
            share[:, h : h + 1] * r[r.shape[0] - 1, :, head_cols(h)].astype(F32)
            for share, r in zip(shares, packs)
        )
        out[:, head_cols(GROUP + h)] = part.astype(BF16)


def small_call(kernel, out_shape, name, *args):
    return pl.pallas_call(
        kernel,
        out_shape=out_shape,
        compiler_params=pltpu.CompilerParams(vmem_limit_bytes=24 * MIB),
        cost_estimate=pl.CostEstimate(flops=10**7, bytes_accessed=2 * 10**6, transcendentals=0),
        name=name,
    )(*args)


def self_kernel(place, starts_ref, query_ref, *refs):
    kv_refs, (out_ref, top_ref, total_ref) = refs[:NX], refs[-3:]
    z, x, earliest = place[0], place[1], place[2]
    first = (NX * z + x) * ROWS
    top_ref[...] = jnp.full_like(top_ref, START)
    total_ref[...] = jnp.zeros_like(total_ref)
    chunks = (z - earliest // (NX * ROWS)) // 2 + 1
    half = GROUP // 2
    blocks = [
        jnp.concatenate([query_ref[:, head_cols(half * n + k)] for k in range(half)], axis=0)
        for n in range(2)
    ]
    for size in range(1, KV_ROWS // 2 + 1):

        @pl.when(chunks == size)
        def _(size=size):
            rows = 2 * size
            column_keys = rows * ROWS
            shape = (ROWS, NX * column_keys)
            step = lax.broadcasted_iota(jnp.int32, shape, 1)
            back = sum((step >= k * column_keys).astype(jnp.int32) for k in range(1, NX))
            inner = step - back * column_keys
            up = inner // ROWS
            column = x - back
            column = jnp.where(column < 0, column + NX, column)
            key_pos = (NX * (z - up) + column) * ROWS + inner - up * ROWS
            row_pos = first + lax.broadcasted_iota(jnp.int32, shape, 0)
            seen = jnp.logical_and(key_pos <= row_pos, key_pos >= starts_ref[:, :1])
            bias = jnp.where(seen, 0.0, LOW)
            bias = jnp.concatenate([bias] * half, axis=0)
            loaded = [ref[r] for ref in kv_refs for r in range(rows)]
            keys = jnp.concatenate([block[:, :HD] for block in loaded], axis=0)
            values = jnp.concatenate([block[:, HD:] for block in loaded], axis=0)
            attend(blocks, keys, values, top_ref, total_ref, bias)

    for h in range(GROUP):
        block = pl.ds(h * ROWS, ROWS)
        out_ref[:, head_cols(h)] = (total_ref[block, :HD] / total_ref[block, HD:]).astype(BF16)


def self_attention(place, starts, queries, kv, earlier):
    vmem = pl.BlockSpec(memory_space=pltpu.VMEM)
    return pl.pallas_call(
        self_kernel,
        grid_spec=pltpu.PrefetchScalarGridSpec(
            num_scalar_prefetch=1,
            grid=(),
            in_specs=[vmem] * (2 + NX) + [pl.BlockSpec(memory_space=pl.ANY)],
            out_specs=vmem,
            scratch_shapes=[
                pltpu.VMEM((GROUP * ROWS, HD), F32),
                pltpu.VMEM((GROUP * ROWS, 2 * HD), F32),
            ],
        ),
        out_shape=jax.ShapeDtypeStruct((ROWS, WIDE), BF16),
        compiler_params=pltpu.CompilerParams(vmem_limit_bytes=48 * MIB),
        cost_estimate=pl.CostEstimate(
            flops=2 * 10**9, bytes_accessed=4 * 10**6, transcendentals=0
        ),
        name="self_attention",
    )(place, starts, queries, *kv, earlier)


def on_device(
    self_queries,
    self_keys,
    self_values,
    cross_queries,
    image_keys,
    image_values,
    image_lists,
    image_counts,
    doc_ids,
):
    span = lax.axis_index("ctx")
    own_docs = lax.dynamic_slice_in_dim(doc_ids, span * ROWS, ROWS)
    starts = jnp.sum((doc_ids[None, :] < own_docs[:, None]).astype(jnp.int32), axis=1)
    place = jnp.stack([span // NX, span % NX, starts[0]]).astype(jnp.int32)
    starts = jnp.broadcast_to(starts[:, None], (ROWS, HD))

    sent = jnp.stack(
        [
            jnp.concatenate([cross_queries[:, :HALF], self_keys], axis=1),
            jnp.concatenate([cross_queries[:, HALF:], self_values], axis=1),
        ]
    )
    own_image = jnp.concatenate([image_keys, image_values], axis=2)
    left, right = moved(own_image, 0, 1), moved(own_image, 0, -1)
    images = {
        "own_key": image_keys,
        "own_value": image_values,
        "left": left,
        "right": right,
        "far_key": moved(left[:, :, :HD], 0, 1),
        "far_value": moved(right[:, :, HD:], 0, -1),
    }
    before, after = [sent], [sent]
    for _ in range(3):
        before.append(moved(before[-1], 1, 0))
        after.append(moved(after[-1], -1, 0))
    far_first = moved(before[3][:1], 1, 0)
    far_second = moved(after[3][1:], -1, 0)

    kv_rows = [(block[0], block[1]) for block in before] + [
        (far_first[0], far_second[0]),
        (after[3][0], after[3][1]),
    ]
    own_kv = jnp.stack([jnp.concatenate([a[:, HALF:], b[:, HALF:]], axis=1) for a, b in kv_rows])
    kv = [own_kv] + [moved(own_kv, 0, k) for k in (1, 2, 3)]

    parts = functools.partial(image_parts, place, image_lists, image_counts, images)
    full = jax.ShapeDtypeStruct((1, ROWS, PACK), BF16)

    def queries_at(distance):
        return [(block[distance], side) for block in (after, before) for side in (0, 1)]

    (near,) = parts((3, NZ - 3), queries_at(3), [], backs=(0, 1, 3))
    plus, minus = parts((4,), [(far_first, 0), (far_second, 0)], [near], halves=True)
    last = [plus, minus]
    plus, minus = moved(plus, 1, 0), moved(minus, -1, 0)
    own = None
    for distance in (3, 2, 1):
        chosen = {"backs": (2,), "start": near} if distance == 3 else {}
        spans, wanted = (distance, NZ - distance), queries_at(distance)
        if distance == 2:
            spans, wanted = spans + (0,), wanted + [(sent, 0), (sent, 1)]
        (local,) = parts(spans, wanted, last, **chosen)
        own = local if distance == 2 else own
        kernel = first_merge_kernel if distance == 3 else merge_kernel
        merged = []
        for side, arrived in enumerate((plus, minus)):
            merged.append(
                small_call(
                    functools.partial(kernel, side), full, f"merge_{distance}_{side}", arrived, local
                )
            )
        plus, minus = moved(merged[0], 1, 0), moved(merged[1], -1, 0)
        last = merged
    self_out = self_attention(place, starts, self_queries, kv, merged[0])
    both = small_call(
        last_merge_kernel,
        jax.ShapeDtypeStruct((ROWS, 2 * WIDE), BF16),
        "merge_0",
        plus,
        minus,
        own,
        self_out,
    )
    back = lax.all_to_all(
        both.reshape(GROUP, ROWS // GROUP, 2 * WIDE), "head", split_axis=0, concat_axis=0
    )
    return tuple(
        jnp.swapaxes(back[:, :, k * WIDE : (k + 1) * WIDE], 0, 1).reshape(
            ROWS // GROUP, GROUP * WIDE
        )
        for k in range(2)
    )


def solution(mesh):
    in_specs = (
        P("ctx", "head"),
        P("ctx", "head"),
        P("ctx", "head"),
        P("ctx", "head"),
        P("ctx", None, "head"),
        P("ctx", None, "head"),
        P(),
        P(),
        P(),
    )
    out_specs = (P(("ctx", "head"), None), P(("ctx", "head"), None))
    return jax.shard_map(
        on_device, mesh=mesh, in_specs=in_specs, out_specs=out_specs, check_vma=False
    )
```
